32 devices in a mesh: lon: 4 (over z), lat: 4 (over y, core), batch: 2 (over x).
Axes of the slice: x: 2, y: 2, z: 4, core: 2. Of those that a mesh axis runs over, the one named last changes fastest.
Arguments:
- attn_input: bfloat16 [16, 24, 48, 192], P('batch', 'lat', 'lon'), parts along dimension 0, may hold values from -6 to 6
- out_grad: bfloat16 [16, 24, 48, 192], P('batch', 'lat', 'lon'), parts along dimension 0, may hold values from -6 to 6
- w_qkv: bfloat16 [192, 576], replicated, may hold values from -0.4375 to 0.4375
- w_proj: bfloat16 [192, 192], replicated, may hold values from -0.4375 to 0.4375
- bias_table: float32 [4, 4, 6, 2, 2, 6, 6, 23], P(None, 'lat'), may hold values from -1 to 401
- mask_ids: int32 [16, 24, 48], P('batch', 'lat', 'lon'), parts along dimension 0, may hold values from 0 to 2
- valid_rows: int32 [2], P('batch'), parts along dimension 0, may hold values from 12 to 24
Outputs:
- grad_input: bfloat16 [16, 24, 48, 192], P('batch', 'lat', 'lon'), parts along dimension 0
- grad_qkv: float32 [384, 576], P('batch'), parts along dimension 0
- grad_proj: float32 [384, 192], P('batch'), parts along dimension 0
- grad_bias: float32 [8, 4, 6, 2, 2, 6, 6, 23], P('batch', 'lat'), parts along dimension 0
The draws below stay inside these ranges and needn't reach their ends.
There are 2 independent parts, one for each index of `batch`. The reference program is written for one: setup_inputs(seed, part) draws one part's arguments, and reference() takes and returns one part's arrays. A program takes and returns all parts, laid end to end along the dimension named above; an argument that names none is the same for every part. Nothing has to cross between parts.
All inputs are finite; a program needn't handle non-finite values.
Results may differ from the reference program's by a relative error of at most 0.0075.
Values may be sent and summed in bfloat16 or wider, within the bound.
A program may use at most 192 MiB of HBM per device.

```python
import jax
import jax.numpy as jnp
from jax import lax

C = 192
HEADS = 6
HEAD_DIM = 32
Z = 8
WZ = 2
WLAT = 6
WLON = 12
WIN = 144
LAT = 24
LON = 48
ZWIN = 4
LATWIN = 4


def draw_bias_table(key, part):
    key = jax.random.fold_in(key, 11)
    base_key = jax.random.fold_in(key, 0)
    shape = (ZWIN, LATWIN, HEADS, WZ, WZ, WLAT, WLAT, 2 * WLON - 1)
    return 0.5 * jnp.clip(jax.random.normal(base_key, shape, jnp.float32), -2.0, 2.0)


def place_ends(drawn, rng, smallest, top_value):
    longest = drawn.shape.index(max(drawn.shape))
    spots = []
    for shift in (0, 1):
        where = [jax.random.randint(jax.random.fold_in(rng, axis), (), 0, length) for axis, length in enumerate(drawn.shape)]
        where[longest] = (where[longest] + shift) % drawn.shape[longest]
        spots.append(tuple(where))
    return drawn.at[spots[0]].set(smallest).at[spots[1]].set(top_value)


def block_scale(stream_key, extent, cuts, low, largest):
    factor_of, own = 1.0, jax.random.fold_in(stream_key, 6)
    for axis_at, parts in cuts:
        draws = jnp.exp(jax.random.uniform(jax.random.fold_in(own, axis_at), (parts,), jnp.float32, low / len(cuts), largest / len(cuts)))
        factor_of = factor_of * jnp.repeat(draws, extent[axis_at] // parts).reshape([-1 if axis == axis_at else 1 for axis in range(len(extent))])
    return factor_of


def scatter_about(rng, extent, deviation, most, shards=(), kind=jnp.bfloat16):
    factor_of = block_scale(rng, extent, shards, -0.22, 0.18) if shards else 1.0
    array = jax.random.normal(rng, extent, jnp.float32) * deviation * factor_of
    return jnp.minimum(jnp.maximum(array, -most), most).astype(kind)


def setup_inputs(seed: int = 0, part: int = 0) -> dict:
    splits = jax.random.split(jax.random.key(seed), 8)
    part_keys = jax.random.split(jax.random.fold_in(splits[7], part), 8)
    attn_input = scatter_about(part_keys[0], (Z, LAT, LON, C), 1.0, 6.0, ((1, 4), (2, 4)))
    out_grad = scatter_about(part_keys[1], (Z, LAT, LON, C), 1.0, 6.0, ((1, 4), (2, 4)))
    w_qkv = scatter_about(splits[2], (C, 3 * C), C ** -0.5, 0.4375)
    w_proj = scatter_about(splits[3], (C, C), C ** -0.5, 0.4375)
    bias_table = draw_bias_table(jax.random.fold_in(splits[7], 71), part)
    mask_ids = place_ends(jax.random.randint(part_keys[5], (Z, LAT, LON), 0, 3), jax.random.fold_in(part_keys[5], 1), 0, 2).astype(jnp.int32)
    valid_rows = jax.random.randint(part_keys[6], (1,), LAT // 2, LAT + 1).astype(jnp.int32)
    return {"attn_input": attn_input, "out_grad": out_grad, "w_qkv": w_qkv, "w_proj": w_proj, "bias_table": bias_table, "mask_ids": mask_ids, "valid_rows": valid_rows}


masked_score = -1.0e9


def narrow(tensor):
    return lax.optimization_barrier(tensor.astype(jnp.bfloat16))


def lon_table():
    column = jnp.arange(WLON, dtype=jnp.int32)
    offset = jnp.arange(2 * WLON - 1, dtype=jnp.int32)
    return (column[:, None, None] - column[None, :, None] + (WLON - 1) == offset[None, None, :]).astype(jnp.float32)


def expand_bias(folded):
    expanded = jnp.einsum("...hxyuvr,abr->...hxuayvb", folded, lon_table(), precision=lax.Precision.HIGHEST)
    return expanded.reshape(expanded.shape[:-7] + (HEADS, WIN, WIN))


def fold_bias(grads):
    divided = grads.reshape(grads.shape[:-3] + (HEADS, WZ, WLAT, WLON, WZ, WLAT, WLON))
    return jnp.einsum("...hxuayvb,abr->...hxyuvr", divided, lon_table(), precision=lax.Precision.HIGHEST)


def to_windows(grid_field):
    levels, lat_rows, lon_cols = grid_field.shape[:3]
    trailing = grid_field.shape[3:]
    divided = grid_field.reshape((levels // WZ, WZ, lat_rows // WLAT, WLAT, lon_cols // WLON, WLON) + trailing)
    arrangement = (0, 2, 4, 1, 3, 5) + tuple(range(6, 6 + len(trailing)))
    return divided.transpose(arrangement).reshape((levels // WZ, lat_rows // WLAT, lon_cols // WLON, WIN) + trailing)


def from_windows(windows, levels, lat_rows, lon_cols):
    trailing = windows.shape[4:]
    divided = windows.reshape((levels // WZ, lat_rows // WLAT, lon_cols // WLON, WZ, WLAT, WLON) + trailing)
    arrangement = (0, 3, 1, 4, 2, 5) + tuple(range(6, 6 + len(trailing)))
    return divided.transpose(arrangement).reshape((levels, lat_rows, lon_cols) + trailing)


def window_backward(shifted, grads_y, allowed, bias, w_qkv, w_proj):
    groups = shifted.shape[0]
    flattened = shifted.reshape(groups * WIN, C)
    projected = jnp.dot(flattened, w_qkv, preferred_element_type=jnp.float32).astype(jnp.bfloat16)
    projected = projected.reshape(groups, WIN, 3, HEADS, HEAD_DIM).astype(jnp.float32)
    query_rows = projected[:, :, 0]
    key_rows = projected[:, :, 1]
    value_rows = projected[:, :, 2]
    temper = HEAD_DIM ** -0.5
    scores = jnp.einsum("gnhd,gmhd->ghnm", query_rows, key_rows) * temper + bias
    scores = jnp.where(allowed[:, None], scores, masked_score)
    exponent = jnp.exp(scores - jnp.max(scores, axis=-1, keepdims=True))
    attn_probs = exponent / jnp.sum(exponent, axis=-1, keepdims=True)
    probs_low = narrow(attn_probs).astype(jnp.float32)
    attended = jnp.einsum("ghnm,gmhd->gnhd", probs_low, value_rows).astype(jnp.bfloat16).reshape(groups * WIN, C)
    upstream = grads_y.reshape(groups * WIN, C)
    grad_proj = jnp.dot(attended.T, upstream, preferred_element_type=jnp.float32)
    grad_att = jnp.dot(upstream, w_proj.T, preferred_element_type=jnp.float32)
    grad_att = narrow(grad_att).astype(jnp.float32).reshape(groups, WIN, HEADS, HEAD_DIM)
    grad_prob = jnp.einsum("gnhd,gmhd->ghnm", grad_att, value_rows)
    grad_score = attn_probs * (grad_prob - jnp.sum(attn_probs * grad_prob, axis=-1, keepdims=True))
    scaled = narrow(grad_score * temper).astype(jnp.float32)
    grad_query = jnp.einsum("ghnm,gmhd->gnhd", scaled, key_rows)
    grad_key = jnp.einsum("ghnm,gnhd->gmhd", scaled, query_rows)
    grad_value = jnp.einsum("ghnm,gnhd->gmhd", probs_low, grad_att)
    grad_rows = jnp.stack([grad_query, grad_key, grad_value], axis=2).astype(jnp.bfloat16).reshape(groups * WIN, 3 * C)
    weight_qkv = jnp.dot(flattened.T, grad_rows, preferred_element_type=jnp.float32)
    grad_shifted = jnp.dot(grad_rows, w_qkv.T, preferred_element_type=jnp.float32).astype(jnp.bfloat16)
    return grad_shifted.reshape(groups, WIN, C), weight_qkv, grad_proj, grad_score


def shift_forward(grid_field):
    grid_field = jnp.roll(grid_field, -(WZ // 2), axis=0)
    grid_field = jnp.roll(grid_field, -(WLON // 2), axis=2)
    filler = jnp.zeros_like(grid_field[:, :WLAT // 2])
    return jnp.concatenate([grid_field[:, WLAT // 2:], filler], axis=1)


def shift_backward(grid_field):
    filler = jnp.zeros_like(grid_field[:, :WLAT // 2])
    grid_field = jnp.concatenate([filler, grid_field[:, :grid_field.shape[1] - WLAT // 2]], axis=1)
    grid_field = jnp.roll(grid_field, WLON // 2, axis=2)
    return jnp.roll(grid_field, WZ // 2, axis=0)


def reference(attn_input, out_grad, w_qkv, w_proj, bias_table, mask_ids, valid_rows):
    levels, lat_rows, lon_cols, channels = attn_input.shape
    shifted = to_windows(shift_forward(attn_input))
    grads_y = to_windows(shift_forward(out_grad))
    anchor = jnp.arange(lat_rows, dtype=jnp.int32) + WLAT // 2
    usable = jnp.broadcast_to((anchor < valid_rows[0])[None, :, None], (levels, lat_rows, lon_cols))
    regions = to_windows(mask_ids)
    usable_win = to_windows(usable)
    allowed = (regions[..., :, None] == regions[..., None, :]) & usable_win[..., None, :]
    allowed = allowed | jnp.eye(WIN, dtype=bool)
    bias_full = expand_bias(bias_table)
    level_wins, lat_wins, lon_wins = shifted.shape[:3]

    def regroup(windows):
        rotated = jnp.moveaxis(windows, 1, 0)
        return rotated.reshape((lat_wins, level_wins * lon_wins) + windows.shape[3:])

    def one_band(pieces):
        band_input, band_grads, band_mask, band_bias = pieces
        expanded = jnp.broadcast_to(band_bias[:, None], (level_wins, lon_wins, HEADS, WIN, WIN))
        expanded = expanded.reshape(level_wins * lon_wins, HEADS, WIN, WIN)
        grad_in, weight_qkv, weight_proj, grad_score = window_backward(band_input, band_grads, band_mask, expanded, w_qkv, w_proj)
        folded = fold_bias(jnp.sum(grad_score.reshape(level_wins, lon_wins, HEADS, WIN, WIN), axis=1))
        return grad_in, weight_qkv, weight_proj, folded

    grad_in, weight_qkv, weight_proj, folded = lax.map(one_band, (regroup(shifted), regroup(grads_y), regroup(allowed), jnp.moveaxis(bias_full, 1, 0)))
    grad_in = jnp.moveaxis(grad_in.reshape((lat_wins, level_wins, lon_wins, WIN, channels)), 0, 1)
    grad_input = shift_backward(from_windows(grad_in, levels, lat_rows, lon_cols))
    factor = (levels * lat_rows * lon_cols) ** -0.5
    grad_qkv = jnp.sum(weight_qkv, axis=0) * factor
    grad_proj = jnp.sum(weight_proj, axis=0) * factor
    return grad_input, grad_qkv, grad_proj, jnp.moveaxis(folded, 0, 1)
```

```python
import functools

import jax
import jax.numpy as jnp
import numpy as np
from jax import lax
from jax.experimental import pallas as pl
from jax.experimental.pallas import tpu as pltpu
from jax.sharding import PartitionSpec as P

C = 192
HEADS = 6
HEAD_DIM = 32
WZ = 2
WLAT = 6
WLON = 12
WIN = 144


masked_score = -1000000000.0


def from_behind(shard, axis, by):
    devices = lax.axis_size(axis)
    return lax.ppermute(shard, axis, [(i, (i + by) % devices) for i in range(devices)])


def shifted_2(shard, axis, by):
    devices = lax.axis_size(axis)
    pairs = [(i, i + by) for i in range(devices) if 0 <= i + by < devices]
    return lax.ppermute(shard, axis, pairs)


def lon_table():
    column = jnp.arange(WLON, dtype=jnp.int32)
    offset = jnp.arange(2 * WLON - 1, dtype=jnp.int32)
    return (
        column[:, None, None] - column[None, :, None] + (WLON - 1) == offset[None, None, :]
    ).astype(jnp.float32)


def expand_bias(folded):
    expanded = jnp.einsum(
        "...hxyuvr,abr->...hxuayvb", folded, lon_table(), precision=lax.Precision.HIGHEST
    )
    return expanded.reshape(expanded.shape[:-7] + (HEADS, WIN, WIN))


def fold_bias(grads):
    divided = grads.reshape(grads.shape[:-3] + (HEADS, WZ, WLAT, WLON, WZ, WLAT, WLON))
    return jnp.einsum(
        "...hxuayvb,abr->...hxyuvr", divided, lon_table(), precision=lax.Precision.HIGHEST
    )


def to_windows(grid_field):
    levels, lat_rows, lon_cols = grid_field.shape[:3]
    trailing = grid_field.shape[3:]
    divided = grid_field.reshape(
        (levels // WZ, WZ, lat_rows // WLAT, WLAT, lon_cols // WLON, WLON) + trailing
    )
    arrangement = (0, 2, 4, 1, 3, 5) + tuple(range(6, 6 + len(trailing)))
    return divided.transpose(arrangement).reshape(
        (levels // WZ, lat_rows // WLAT, lon_cols // WLON, WIN) + trailing
    )


def from_windows(windows, levels, lat_rows, lon_cols):
    trailing = windows.shape[4:]
    divided = windows.reshape(
        (levels // WZ, lat_rows // WLAT, lon_cols // WLON, WZ, WLAT, WLON) + trailing
    )
    arrangement = (0, 3, 1, 4, 2, 5) + tuple(range(6, 6 + len(trailing)))
    return divided.transpose(arrangement).reshape((levels, lat_rows, lon_cols) + trailing)


def outer_part(grid_field, cut_width, axis, leading):
    length = grid_field.shape[axis]
    if leading:
        return lax.slice_in_dim(grid_field, 0, cut_width, axis=axis)
    return lax.slice_in_dim(grid_field, length - cut_width, length, axis=axis)


def inner_part(grid_field, cut_width, axis, leading):
    length = grid_field.shape[axis]
    if leading:
        return lax.slice_in_dim(grid_field, cut_width, length, axis=axis)
    return lax.slice_in_dim(grid_field, 0, length - cut_width, axis=axis)


def attach(kept, arrived, axis, leading):
    if leading:
        return jnp.concatenate([kept, arrived], axis=axis)
    return jnp.concatenate([arrived, kept], axis=axis)


def displace(fields, heading):
    leading = heading < 0
    fields = [jnp.roll(grid_field, heading * (WZ // 2), axis=0) for grid_field in fields]
    border = jnp.stack([outer_part(grid_field, WLON // 2, 2, leading) for grid_field in fields])
    arrived = from_behind(border, "lon", heading)
    fields = [
        attach(inner_part(grid_field, WLON // 2, 2, leading), arrived[number], 2, leading)
        for number, grid_field in enumerate(fields)
    ]
    border = jnp.stack([outer_part(grid_field, WLAT // 2, 1, leading) for grid_field in fields])
    arrived = shifted_2(border, "lat", heading)
    return [
        attach(inner_part(grid_field, WLAT // 2, 1, leading), arrived[number], 1, leading)
        for number, grid_field in enumerate(fields)
    ]


def window_backward(shifted, grads_y, allowed, bias, w_qkv, w_proj):
    groups = shifted.shape[0]
    flattened = shifted.reshape(groups * WIN, C)
    projected = jnp.dot(flattened, w_qkv, preferred_element_type=jnp.float32).astype(jnp.bfloat16)
    projected = projected.reshape(groups, WIN, 3, HEADS, HEAD_DIM)
    query_rows = projected[:, :, 0]
    key_rows = projected[:, :, 1]
    value_rows = projected[:, :, 2]
    temper = HEAD_DIM ** (-0.5)
    scores = (
        jnp.einsum("gnhd,gmhd->ghnm", query_rows, key_rows, preferred_element_type=jnp.float32)
        * temper
        + bias
    )
    scores = jnp.where(allowed[:, None], scores, masked_score)
    exponent = jnp.exp(scores - jnp.max(scores, axis=-1, keepdims=True))
    attn_probs = exponent / jnp.sum(exponent, axis=-1, keepdims=True)
    probs_low = attn_probs.astype(jnp.bfloat16)
    attended = jnp.einsum(
        "ghnm,gmhd->gnhd", probs_low, value_rows, preferred_element_type=jnp.float32
    )
    attended = attended.astype(jnp.bfloat16).reshape(groups * WIN, C)
    upstream = grads_y.reshape(groups * WIN, C)
    grad_proj = jnp.einsum("tc,te->ce", attended, upstream, preferred_element_type=jnp.float32)
    grad_att = jnp.einsum("te,ce->tc", upstream, w_proj, preferred_element_type=jnp.float32)
    grad_att = grad_att.astype(jnp.bfloat16).reshape(groups, WIN, HEADS, HEAD_DIM)
    grad_prob = jnp.einsum(
        "gnhd,gmhd->ghnm", grad_att, value_rows, preferred_element_type=jnp.float32
    )
    grad_score = attn_probs * (grad_prob - jnp.sum(attn_probs * grad_prob, axis=-1, keepdims=True))
    scaled = (grad_score * temper).astype(jnp.bfloat16)
    grad_query = jnp.einsum("ghnm,gmhd->gnhd", scaled, key_rows, preferred_element_type=jnp.float32)
    grad_key = jnp.einsum("ghnm,gnhd->gmhd", scaled, query_rows, preferred_element_type=jnp.float32)
    grad_value = jnp.einsum(
        "ghnm,gnhd->gmhd", probs_low, grad_att, preferred_element_type=jnp.float32
    )
    grad_rows = (
        jnp.stack([grad_query, grad_key, grad_value], axis=2)
        .astype(jnp.bfloat16)
        .reshape(groups * WIN, 3 * C)
    )
    weight_qkv = jnp.einsum("tc,te->ce", flattened, grad_rows, preferred_element_type=jnp.float32)
    grad_shifted = jnp.einsum(
        "te,ce->tc", grad_rows, w_qkv, preferred_element_type=jnp.float32
    ).astype(jnp.bfloat16)
    return (grad_shifted.reshape(groups, WIN, C), weight_qkv, grad_proj, grad_score)


def body(attn_input, out_grad, w_qkv, w_proj, bias_table, mask_ids, valid_rows):
    levels, lat_rows, lon_cols, channels = attn_input.shape
    moved_input, moved_grad = displace([attn_input, out_grad], -1)
    shifted = to_windows(moved_input)
    grads_y = to_windows(moved_grad)
    anchor = jnp.arange(lat_rows, dtype=jnp.int32) + lax.axis_index("lat") * lat_rows + WLAT // 2
    usable = jnp.broadcast_to((anchor < valid_rows[0])[None, :, None], (levels, lat_rows, lon_cols))
    regions = to_windows(mask_ids)
    usable_win = to_windows(usable)
    allowed = (regions[..., :, None] == regions[..., None, :]) & usable_win[..., None, :]
    allowed = allowed | jnp.eye(WIN, dtype=bool)
    bias_full = expand_bias(bias_table)
    level_wins, lat_wins, lon_wins = shifted.shape[:3]

    def regroup(windows):
        rotated = jnp.moveaxis(windows, 1, 0)
        return rotated.reshape((lat_wins, level_wins * lon_wins) + windows.shape[3:])

    def one_band(pieces):
        band_input, band_grads, band_mask, band_bias = pieces
        expanded = band_bias[:, None]
        expanded = expanded.reshape(level_wins * lon_wins, HEADS, WIN, WIN)
        grad_in, weight_qkv, weight_proj, grad_score = window_backward(
            band_input, band_grads, band_mask, expanded, w_qkv, w_proj
        )
        folded = fold_bias(
            jnp.sum(grad_score.reshape(level_wins, lon_wins, HEADS, WIN, WIN), axis=1)
        )
        return (grad_in, weight_qkv, weight_proj, folded)

    grad_in, weight_qkv, weight_proj, folded = lax.map(
        one_band,
        (regroup(shifted), regroup(grads_y), regroup(allowed), jnp.moveaxis(bias_full, 1, 0)),
    )
    grad_in = jnp.moveaxis(grad_in.reshape((lat_wins, level_wins, lon_wins, WIN, channels)), 0, 1)
    grad_input = displace([from_windows(grad_in, levels, lat_rows, lon_cols)], 1)[0]
    local_qkv = jnp.sum(weight_qkv, axis=0)
    local_proj = jnp.sum(weight_proj, axis=0)
    local_table = jnp.moveaxis(folded, 0, 1)
    total_qkv, total_proj = lax.psum((local_qkv, local_proj), ("lon", "lat"))
    grad_bias = lax.psum(local_table, "lon")
    cells = levels * lat_rows * lax.axis_size("lat") * lon_cols * lax.axis_size("lon")
    factor = cells ** (-0.5)
    return (grad_input, total_qkv * factor, total_proj * factor, grad_bias)

BANDS = 16
PAD = 48
COLS = 16


def place_maps():
    send = np.zeros((4 * PAD, WZ * WLAT * COLS), np.float32)
    order = np.zeros((WIN, 4 * PAD), np.float32)
    for a in range(WZ):
        for b in range(WLAT // 2):
            for c in range(WLON // 2):
                for part in range(4):
                    low_row, low_col = part // 2, part % 2
                    spot = part * PAD + a * 18 + b * 6 + c
                    row = b + (0 if low_row else 3)
                    col = c + (0 if low_col else 6)
                    send[spot, (a * WLAT + row) * COLS + col] = 1.0
                    win_row = b + (3 if low_row else 0)
                    win_col = c + (6 if low_col else 0)
                    order[win_col * 12 + a * WLAT + win_row, spot] = 1.0
    return send, order


def bias_map():
    spread = np.zeros((276, 384), np.float32)
    for pair in range(12):
        for d in range(23):
            spread[pair * 23 + d, (22 - d) * 12 + pair] = 1.0
    return spread


def dot_nn(a, b):
    return lax.dot_general(a, b, (((1,), (0,)), ((), ())), preferred_element_type=jnp.float32)


def dot_nt(a, b):
    return lax.dot_general(a, b, (((1,), (1,)), ((), ())), preferred_element_type=jnp.float32)


def dot_tn(a, b):
    return lax.dot_general(a, b, (((0,), (0,)), ((), ())), preferred_element_type=jnp.float32)


def kernel(
    factor, x_ref, g_ref, wq_ref, wp_ref, tab_ref, idr_ref, idc_ref,
    p1_ref, p1t_ref, p2_ref, p2t_ref, gm_ref, gmt_ref,
    out_x, out_w, out_p, out_b,
    xs, sb, rb, hs, hr, bias, tp, fold, dsr, xa, ga, aa, gr, dw,
    ws, wr, wl, wm, wf, wg, bs, br, bg, bo,
    halo_send, halo_recv, back_send, back_recv, bsum_send, bsum_recv, ball_send, ball_recv,
    wa_send, wa_recv, wb_send, wb_recv, wc_send, wc_recv, wd_send, wd_recv,
):
    f32, bf16 = jnp.float32, jnp.bfloat16
    lon, lat = lax.axis_index("lon"), lax.axis_index("lat")
    nl, nt = 4, 4

    def at(dlon, dlat):
        return {"lon": lax.rem(lon + dlon + nl, nl), "lat": lax.rem(lat + dlat + nt, nt)}

    def remote(src, dst, send, recv, where):
        return pltpu.make_async_remote_copy(
            src_ref=src, dst_ref=dst, send_sem=send, recv_sem=recv,
            device_id=where, device_id_type=pl.DeviceIdType.MESH,
        )

    barrier = pltpu.get_barrier_semaphore()
    friends = [(1, 0), (2, 0), (3, 0), (0, 1), (0, 2), (0, 3), (1, 1), (-1, -1)]
    for dlon, dlat in friends:
        pl.semaphore_signal(
            barrier, inc=1, device_id=at(dlon, dlat), device_id_type=pl.DeviceIdType.MESH
        )

    xs[...] = jnp.zeros_like(xs)
    for arr, ref in enumerate((x_ref, g_ref)):
        for z in range(8):
            for r in range(6):
                xs[arr, z, COLS * r : COLS * r + 12, :] = ref[z, r]
    p1 = p1_ref[...]
    for i in range(4):
        for arr in range(2):
            block = jnp.concatenate([xs[arr, (2 * i + 1) % 8], xs[arr, (2 * i + 2) % 8]], axis=0)
            cut = dot_nn(p1, block).astype(bf16)
            rb[0, arr, i] = cut[0:PAD]
            for part in range(1, 4):
                sb[part - 1, arr, i] = cut[part * PAD : (part + 1) * PAD]
    pl.semaphore_wait(barrier, len(friends))
    halo = [
        remote(sb.at[n], rb.at[n + 1], halo_send.at[n], halo_recv.at[n], at(*where))
        for n, where in enumerate(((-1, 0), (0, -1), (-1, -1)))
    ]
    for copy in halo:
        copy.start()

    def expand(i, carry):
        table = tab_ref[i]
        top = table.astype(bf16)
        rest = table - top.astype(f32)
        mid = rest.astype(bf16)
        low = (rest - mid.astype(f32)).astype(bf16)
        spread = gm_ref[...]
        tp[...] = dot_nn(top, spread) + dot_nn(mid, spread) + dot_nn(low, spread)
        for h in range(HEADS):
            for c in range(12):
                bias[i, h, 12 * c : 12 * c + 12, :] = tp[
                    16 * h : 16 * h + 12, 12 * (11 - c) : 12 * (11 - c) + WIN
                ]
        return carry

    lax.fori_loop(0, 4, expand, 0)
    for n in range(16):
        ws[n] = jnp.zeros((16, 768), bf16)
    for copy in halo:
        copy.wait()

    spot = lax.broadcasted_iota(jnp.int32, (1, 4 * PAD), 1)
    far = spot >= 2 * PAD
    last_row = lat == nt - 1
    first_row = lat == 0
    p2 = p2_ref[...] * jnp.where(far & last_row, 0.0, 1.0).astype(bf16)
    p1t = p1t_ref[...] * jnp.where(far & first_row, 0.0, 1.0).astype(bf16)
    rows = lax.broadcasted_iota(jnp.int32, (WIN, WIN), 0)
    cols = lax.broadcasted_iota(jnp.int32, (WIN, WIN), 1)
    same = rows == cols
    temper = HEAD_DIM ** (-0.5)

    def bias_copy(s):
        w = lax.rem(lon + 1 + s, nl)
        return remote(bs.at[w], br.at[s], bsum_send.at[s], bsum_recv.at[s], at(1 + s, 0))

    def window(s, carry):
        w = lax.rem(lon + 1 + s, nl)
        x4 = jnp.concatenate([rb[part, 0, w] for part in range(4)], axis=0)
        g4 = jnp.concatenate([rb[part, 1, w] for part in range(4)], axis=0)
        x = dot_nn(p2, x4).astype(bf16)
        g = dot_nn(p2, g4).astype(bf16)
        xa[w] = x
        ga[w] = g
        qkv = dot_nn(x, wq_ref[...]).astype(bf16)
        gatt = dot_nt(g, wp_ref[...]).astype(bf16)
        allowed = (idc_ref[w] == idr_ref[w]) | same
        fold[...] = jnp.zeros_like(fold)
        for h in range(HEADS):
            lo = HEAD_DIM * h
            q = qkv[:, lo : lo + 32]
            k = qkv[:, C + lo : C + lo + 32]
            v = qkv[:, 2 * C + lo : 2 * C + lo + 32]
            go = gatt[:, lo : lo + 32]
            scores = dot_nt(q, k) * temper + bias[w, h]
            scores = jnp.where(allowed, scores, masked_score)
            power = jnp.exp(scores - jnp.max(scores, axis=-1, keepdims=True))
            probs = power / jnp.sum(power, axis=-1, keepdims=True)
            low = probs.astype(bf16)
            aa[w, :, lo : lo + 32] = dot_nn(low, v).astype(bf16)
            gp = dot_nt(go, v)
            gs = probs * (gp - jnp.sum(probs * gp, axis=-1, keepdims=True))
            dsr[h] = gs
            scaled = (gs * temper).astype(bf16)
            gr[w, :, lo : lo + 32] = dot_nn(scaled, k).astype(bf16)
            gr[w, :, C + lo : C + lo + 32] = dot_tn(scaled, q).astype(bf16)
            gr[w, :, 2 * C + lo : 2 * C + lo + 32] = dot_tn(low, go).astype(bf16)
            for c in range(12):
                off = 12 * (11 - c)
                fold[16 * h : 16 * h + 12, off : off + WIN] += dsr[h, 12 * c : 12 * c + 12, :]
        back = dot_nt(gr[w], wq_ref[...]).astype(bf16)
        cut = dot_nn(p2t_ref[...], back).astype(bf16)
        for part in range(4):
            hs[part, w] = cut[part * PAD : (part + 1) * PAD]
        bs[w] = dot_nn(fold[...].astype(bf16), gmt_ref[...]).astype(bf16)

        @pl.when(s < 3)
        def _():
            bias_copy(s).start()

        return carry

    lax.fori_loop(0, 4, window, 0)

    home = [
        remote(hs.at[n + 1], hr.at[n], back_send.at[n], back_recv.at[n], at(*where))
        for n, where in enumerate(((1, 0), (0, 1), (1, 1)))
    ]
    for copy in home:
        copy.start()

    dw[:, :576] = dot_tn(xa[...].reshape(576, C), gr[...].reshape(576, 576))
    dw[:, 576:] = dot_tn(aa[...].reshape(576, C), ga[...].reshape(576, C))
    for n in range(16):
        ws[n, 0:12, :] = dw[12 * n : 12 * n + 12, :].astype(bf16)
    wa = []
    for d in range(1, 4):
        to = lax.rem(lat + d, nt)
        wa.append(
            remote(ws.at[pl.ds(4 * to, 4)], wr.at[d - 1], wa_send.at[d - 1], wa_recv.at[d - 1], at(0, d))
        )
    for copy in wa:
        copy.start()

    for s in range(3):
        bias_copy(s).wait()
    total = bs[lon].astype(f32)
    for s in range(3):
        total = total + br[s].astype(f32)
    bg[...] = total.astype(bf16)
    ball = [
        remote(bg, bo.at[lon], ball_send.at[d - 1], ball_recv.at[d - 1], at(d, 0))
        for d in range(1, 4)
    ]
    for copy in ball:
        copy.start()

    for copy in wa:
        copy.wait()
    part_sum = ws[pl.ds(4 * lat, 4)].astype(f32)
    for d in range(3):
        part_sum = part_sum + wr[d].astype(f32)
    wl[...] = part_sum.astype(bf16)
    wb = []
    for d in range(1, 4):
        to = lax.rem(lon + d, nl)
        wb.append(
            remote(wl.at[to], wm.at[d - 1], wb_send.at[d - 1], wb_recv.at[d - 1], at(d, 0))
        )
    for copy in wb:
        copy.start()

    for copy in home:
        copy.wait()
    for i in range(4):
        y4 = jnp.concatenate([hs[0, i]] + [hr[n, i] for n in range(3)], axis=0)
        y = dot_nn(p1t, y4).astype(bf16)
        for a in range(2):
            z = (2 * i + 1 + a) % 8
            for r in range(6):
                row = (a * 6 + r) * COLS
                out_x[z, r] = y[row : row + 12]

    for copy in wb:
        copy.wait()
    mine = wl[lon].astype(f32)
    for d in range(3):
        mine = mine + wm[d].astype(f32)
    wf[...] = mine.astype(bf16)
    wg[4 * lat + lon] = wf[...]
    wc = [
        remote(wf, wg.at[4 * lat + lon], wc_send.at[d - 1], wc_recv.at[d - 1], at(d, 0))
        for d in range(1, 4)
    ]
    for copy in wc:
        copy.start()
    for copy in wc:
        copy.wait()
    own = wg.at[pl.ds(4 * lat, 4)]
    wd = [
        remote(own, own, wd_send.at[d - 1], wd_recv.at[d - 1], at(0, d))
        for d in range(1, 4)
    ]
    for copy in wd:
        copy.start()

    for copy in ball:
        copy.wait()
    bo[lon] = bg[...]
    out_b[...] = bo[...].astype(f32)

    for copy in wd:
        copy.wait()
    for n in range(16):
        piece = wg[n].astype(f32) * factor
        out_w[12 * n : 12 * n + 12, :] = piece[0:12, :576]
        out_p[12 * n : 12 * n + 12, :] = piece[0:12, 576:]


def fused_body(attn_input, out_grad, w_qkv, w_proj, bias_table, mask_ids, valid_rows):
    f32, bf16 = jnp.float32, jnp.bfloat16
    levels, lat_rows, lon_cols, _ = attn_input.shape
    anchor = jnp.arange(lat_rows, dtype=jnp.int32) + lax.axis_index("lat") * lat_rows + WLAT // 2
    usable = (anchor < valid_rows[0])[None, :, None]
    keyed = jnp.where(usable, mask_ids, -1)

    def ordered(ids):
        return ids.reshape(4, 2, 6, 12).transpose(0, 3, 1, 2)

    idc = ordered(mask_ids).reshape(4, WIN, 1)
    idr = ordered(keyed).reshape(4, 1, WIN)
    table = bias_table.reshape(4, 6, 2, 2, 6, 6, 23).transpose(0, 1, 2, 4, 3, 5, 6)
    table = table.reshape(4, 6, 12, 276)
    table = jnp.pad(table, ((0, 0), (0, 0), (0, 4), (0, 0))).reshape(4, 96, 276)
    send, order = place_maps()
    spread = bias_map()
    maps = [jnp.asarray(m, bf16) for m in (send, send.T, order, order.T, spread, spread.T)]
    cells = levels * lat_rows * lax.axis_size("lat") * lon_cols * lax.axis_size("lon")
    vm = pltpu.VMEM
    sem = pltpu.SemaphoreType.DMA((3,))
    scratch = [
        vm((2, 8, 96, C), bf16),
        vm((3, 2, 4, PAD, C), bf16),
        vm((4, 2, 4, PAD, C), bf16),
        vm((4, 4, PAD, C), bf16),
        vm((3, 4, PAD, C), bf16),
        vm((4, HEADS, WIN, WIN), f32),
        vm((96, 384), f32),
        vm((96, 384), f32),
        vm((HEADS, WIN, WIN), f32),
        vm((4, WIN, C), bf16),
        vm((4, WIN, C), bf16),
        vm((4, WIN, C), bf16),
        vm((4, WIN, 3 * C), bf16),
        vm((C, 768), f32),
        vm((16, 16, 768), bf16),
        vm((3, 4, 16, 768), bf16),
        vm((4, 16, 768), bf16),
        vm((3, 16, 768), bf16),
        vm((16, 768), bf16),
        vm((16, 16, 768), bf16),
        vm((4, 96, 276), bf16),
        vm((3, 96, 276), bf16),
        vm((96, 276), bf16),
        vm((4, 96, 276), bf16),
    ] + [sem] * 16
    whole = pl.BlockSpec(memory_space=pltpu.VMEM)
    grad_input, grad_qkv, grad_proj, folded = pl.pallas_call(
        functools.partial(kernel, cells ** (-0.5)),
        out_shape=(
            jax.ShapeDtypeStruct((8, 6, 12, C), bf16),
            jax.ShapeDtypeStruct((C, 3 * C), f32),
            jax.ShapeDtypeStruct((C, C), f32),
            jax.ShapeDtypeStruct((4, 96, 276), f32),
        ),
        in_specs=[whole] * 13,
        out_specs=[whole] * 4,
        scratch_shapes=scratch,
        compiler_params=pltpu.CompilerParams(
            collective_id=0, has_side_effects=True, vmem_limit_bytes=48 * 1024 * 1024
        ),
    )(attn_input, out_grad, w_qkv, w_proj, table, idr, idc, *maps)
    folded = folded.reshape(4, 6, 16, 276)[:, :, :12].reshape(4, 6, 2, 6, 2, 6, 23)
    grad_bias = folded.transpose(0, 1, 2, 4, 3, 5, 6)[:, None]
    return grad_input, grad_qkv, grad_proj, grad_bias


def fitting_body(attn_input, *others):
    tuned = (
        lax.axis_size("lon") == 4
        and lax.axis_size("lat") == 4
        and attn_input.shape == (8, 6, 12, C)
    )
    return (fused_body if tuned else body)(attn_input, *others)


def solution(mesh):
    placed = (
        P("batch", "lat", "lon", None),
        P("batch", "lat", "lon", None),
        P(),
        P(),
        P(None, "lat", None, None, None, None, None, None),
        P("batch", "lat", "lon"),
        P("batch"),
    )
    return jax.shard_map(
        fitting_body,
        mesh=mesh,
        in_specs=placed,
        out_specs=(
            P("batch", "lat", "lon", None),
            P("batch", None),
            P("batch", None),
            P("batch", "lat", None, None, None, None, None, None),
        ),
        check_vma=False,
    )
```

```python
import functools

import jax
import jax.numpy as jnp
import numpy as np
from jax import lax
from jax.experimental import pallas as pl
from jax.experimental.pallas import tpu as pltpu
from jax.sharding import PartitionSpec as P

C = 192
HEADS = 6
HEAD_DIM = 32
WZ = 2
WLAT = 6
WLON = 12
WIN = 144


masked_score = -1000000000.0


def from_behind(shard, axis, by):
    devices = lax.axis_size(axis)
    return lax.ppermute(shard, axis, [(i, (i + by) % devices) for i in range(devices)])


def shifted_2(shard, axis, by):
    devices = lax.axis_size(axis)
    pairs = [(i, i + by) for i in range(devices) if 0 <= i + by < devices]
    return lax.ppermute(shard, axis, pairs)


def lon_table():
    column = jnp.arange(WLON, dtype=jnp.int32)
    offset = jnp.arange(2 * WLON - 1, dtype=jnp.int32)
    return (
        column[:, None, None] - column[None, :, None] + (WLON - 1) == offset[None, None, :]
    ).astype(jnp.float32)


def expand_bias(folded):
    expanded = jnp.einsum(
        "...hxyuvr,abr->...hxuayvb", folded, lon_table(), precision=lax.Precision.HIGHEST
    )
    return expanded.reshape(expanded.shape[:-7] + (HEADS, WIN, WIN))


def fold_bias(grads):
    divided = grads.reshape(grads.shape[:-3] + (HEADS, WZ, WLAT, WLON, WZ, WLAT, WLON))
    return jnp.einsum(
        "...hxuayvb,abr->...hxyuvr", divided, lon_table(), precision=lax.Precision.HIGHEST
    )


def to_windows(grid_field):
    levels, lat_rows, lon_cols = grid_field.shape[:3]
    trailing = grid_field.shape[3:]
    divided = grid_field.reshape(
        (levels // WZ, WZ, lat_rows // WLAT, WLAT, lon_cols // WLON, WLON) + trailing
    )
    arrangement = (0, 2, 4, 1, 3, 5) + tuple(range(6, 6 + len(trailing)))
    return divided.transpose(arrangement).reshape(
        (levels // WZ, lat_rows // WLAT, lon_cols // WLON, WIN) + trailing
    )


def from_windows(windows, levels, lat_rows, lon_cols):
    trailing = windows.shape[4:]
    divided = windows.reshape(
        (levels // WZ, lat_rows // WLAT, lon_cols // WLON, WZ, WLAT, WLON) + trailing
    )
    arrangement = (0, 3, 1, 4, 2, 5) + tuple(range(6, 6 + len(trailing)))
    return divided.transpose(arrangement).reshape((levels, lat_rows, lon_cols) + trailing)


def outer_part(grid_field, cut_width, axis, leading):
    length = grid_field.shape[axis]
    if leading:
        return lax.slice_in_dim(grid_field, 0, cut_width, axis=axis)
    return lax.slice_in_dim(grid_field, length - cut_width, length, axis=axis)


def inner_part(grid_field, cut_width, axis, leading):
    length = grid_field.shape[axis]
    if leading:
        return lax.slice_in_dim(grid_field, cut_width, length, axis=axis)
    return lax.slice_in_dim(grid_field, 0, length - cut_width, axis=axis)


def attach(kept, arrived, axis, leading):
    if leading:
        return jnp.concatenate([kept, arrived], axis=axis)
    return jnp.concatenate([arrived, kept], axis=axis)


def displace(fields, heading):
    leading = heading < 0
    fields = [jnp.roll(grid_field, heading * (WZ // 2), axis=0) for grid_field in fields]
    border = jnp.stack([outer_part(grid_field, WLON // 2, 2, leading) for grid_field in fields])
    arrived = from_behind(border, "lon", heading)
    fields = [
        attach(inner_part(grid_field, WLON // 2, 2, leading), arrived[number], 2, leading)
        for number, grid_field in enumerate(fields)
    ]
    border = jnp.stack([outer_part(grid_field, WLAT // 2, 1, leading) for grid_field in fields])
    arrived = shifted_2(border, "lat", heading)
    return [
        attach(inner_part(grid_field, WLAT // 2, 1, leading), arrived[number], 1, leading)
        for number, grid_field in enumerate(fields)
    ]


def window_backward(shifted, grads_y, allowed, bias, w_qkv, w_proj):
    groups = shifted.shape[0]
    flattened = shifted.reshape(groups * WIN, C)
    projected = jnp.dot(flattened, w_qkv, preferred_element_type=jnp.float32).astype(jnp.bfloat16)
    projected = projected.reshape(groups, WIN, 3, HEADS, HEAD_DIM)
    query_rows = projected[:, :, 0]
    key_rows = projected[:, :, 1]
    value_rows = projected[:, :, 2]
    temper = HEAD_DIM ** (-0.5)
    scores = (
        jnp.einsum("gnhd,gmhd->ghnm", query_rows, key_rows, preferred_element_type=jnp.float32)
        * temper
        + bias
    )
    scores = jnp.where(allowed[:, None], scores, masked_score)
    exponent = jnp.exp(scores - jnp.max(scores, axis=-1, keepdims=True))
    attn_probs = exponent / jnp.sum(exponent, axis=-1, keepdims=True)
    probs_low = attn_probs.astype(jnp.bfloat16)
    attended = jnp.einsum(
        "ghnm,gmhd->gnhd", probs_low, value_rows, preferred_element_type=jnp.float32
    )
    attended = attended.astype(jnp.bfloat16).reshape(groups * WIN, C)
    upstream = grads_y.reshape(groups * WIN, C)
    grad_proj = jnp.einsum("tc,te->ce", attended, upstream, preferred_element_type=jnp.float32)
    grad_att = jnp.einsum("te,ce->tc", upstream, w_proj, preferred_element_type=jnp.float32)
    grad_att = grad_att.astype(jnp.bfloat16).reshape(groups, WIN, HEADS, HEAD_DIM)
    grad_prob = jnp.einsum(
        "gnhd,gmhd->ghnm", grad_att, value_rows, preferred_element_type=jnp.float32
    )
    grad_score = attn_probs * (grad_prob - jnp.sum(attn_probs * grad_prob, axis=-1, keepdims=True))
    scaled = (grad_score * temper).astype(jnp.bfloat16)
    grad_query = jnp.einsum("ghnm,gmhd->gnhd", scaled, key_rows, preferred_element_type=jnp.float32)
    grad_key = jnp.einsum("ghnm,gnhd->gmhd", scaled, query_rows, preferred_element_type=jnp.float32)
    grad_value = jnp.einsum(
        "ghnm,gnhd->gmhd", probs_low, grad_att, preferred_element_type=jnp.float32
    )
    grad_rows = (
        jnp.stack([grad_query, grad_key, grad_value], axis=2)
        .astype(jnp.bfloat16)
        .reshape(groups * WIN, 3 * C)
    )
    weight_qkv = jnp.einsum("tc,te->ce", flattened, grad_rows, preferred_element_type=jnp.float32)
    grad_shifted = jnp.einsum(
        "te,ce->tc", grad_rows, w_qkv, preferred_element_type=jnp.float32
    ).astype(jnp.bfloat16)
    return (grad_shifted.reshape(groups, WIN, C), weight_qkv, grad_proj, grad_score)


def body(attn_input, out_grad, w_qkv, w_proj, bias_table, mask_ids, valid_rows):
    levels, lat_rows, lon_cols, channels = attn_input.shape
    moved_input, moved_grad = displace([attn_input, out_grad], -1)
    shifted = to_windows(moved_input)
    grads_y = to_windows(moved_grad)
    anchor = jnp.arange(lat_rows, dtype=jnp.int32) + lax.axis_index("lat") * lat_rows + WLAT // 2
    usable = jnp.broadcast_to((anchor < valid_rows[0])[None, :, None], (levels, lat_rows, lon_cols))
    regions = to_windows(mask_ids)
    usable_win = to_windows(usable)
    allowed = (regions[..., :, None] == regions[..., None, :]) & usable_win[..., None, :]
    allowed = allowed | jnp.eye(WIN, dtype=bool)
    bias_full = expand_bias(bias_table)
    level_wins, lat_wins, lon_wins = shifted.shape[:3]

    def regroup(windows):
        rotated = jnp.moveaxis(windows, 1, 0)
        return rotated.reshape((lat_wins, level_wins * lon_wins) + windows.shape[3:])

    def one_band(pieces):
        band_input, band_grads, band_mask, band_bias = pieces
        expanded = band_bias[:, None]
        expanded = expanded.reshape(level_wins * lon_wins, HEADS, WIN, WIN)
        grad_in, weight_qkv, weight_proj, grad_score = window_backward(
            band_input, band_grads, band_mask, expanded, w_qkv, w_proj
        )
        folded = fold_bias(
            jnp.sum(grad_score.reshape(level_wins, lon_wins, HEADS, WIN, WIN), axis=1)
        )
        return (grad_in, weight_qkv, weight_proj, folded)

    grad_in, weight_qkv, weight_proj, folded = lax.map(
        one_band,
        (regroup(shifted), regroup(grads_y), regroup(allowed), jnp.moveaxis(bias_full, 1, 0)),
    )
    grad_in = jnp.moveaxis(grad_in.reshape((lat_wins, level_wins, lon_wins, WIN, channels)), 0, 1)
    grad_input = displace([from_windows(grad_in, levels, lat_rows, lon_cols)], 1)[0]
    local_qkv = jnp.sum(weight_qkv, axis=0)
    local_proj = jnp.sum(weight_proj, axis=0)
    local_table = jnp.moveaxis(folded, 0, 1)
    total_qkv, total_proj = lax.psum((local_qkv, local_proj), ("lon", "lat"))
    grad_bias = lax.psum(local_table, "lon")
    cells = levels * lat_rows * lax.axis_size("lat") * lon_cols * lax.axis_size("lon")
    factor = cells ** (-0.5)
    return (grad_input, total_qkv * factor, total_proj * factor, grad_bias)

def place_map():
    order = np.zeros((576, 576), np.float32)
    for i in range(4):
        for c in range(12):
            for a in range(2):
                for b in range(6):
                    order[i * WIN + c * 12 + a * 6 + b, b * 96 + c * 8 + (2 * i + a + 1) % 8] = 1.0
    return order


def bias_map():
    spread = np.zeros((384, 384), np.float32)
    for a in range(2):
        for b in range(6):
            for d in range(23):
                spread[(2 * b + a) * 32 + d, (22 - d) * 12 + a * 6 + b] = 1.0
    return spread


def dot_nn(a, b):
    return lax.dot_general(a, b, (((1,), (0,)), ((), ())), preferred_element_type=jnp.float32)


def dot_nt(a, b):
    return lax.dot_general(a, b, (((1,), (1,)), ((), ())), preferred_element_type=jnp.float32)


def dot_tn(a, b):
    return lax.dot_general(a, b, (((0,), (0,)), ((), ())), preferred_element_type=jnp.float32)


def kernel(
    factor, x_ref, g_ref, wq_ref, wp_ref, tab_ref, ids_ref,
    pm_ref, pt_ref, gm_ref, gmt_ref,
    out_x, out_w, out_p, out_b,
    pk, sg, hs, og, bias, tabx, tp, fold, dsr, xa, ga, aa, gr, qa, ca, dw,
    ws, wr1, w2, wr2, wl, wm, wf, wo, bs, br, bg, bo,
    halo_send, halo_recv, back_send, back_recv, bsum_send, bsum_recv, ball_send, ball_recv,
    wb_send, wb_recv, wc_send, wc_recv, pair_send, pair_recv,
):
    f32, bf16 = jnp.float32, jnp.bfloat16
    lon, lat = lax.axis_index("lon"), lax.axis_index("lat")
    nl, nt = 4, 4
    core, far_y = lax.rem(lat, 2), lat // 2

    def at(dlon, dlat):
        return {"lon": lax.rem(lon + dlon + nl, nl), "lat": lax.rem(lat + dlat + nt, nt)}

    def remote(src, dst, send, recv, where):
        return pltpu.make_async_remote_copy(
            src_ref=src, dst_ref=dst, send_sem=send, recv_sem=recv,
            device_id=where, device_id_type=pl.DeviceIdType.MESH,
        )

    barrier = pltpu.get_barrier_semaphore()
    friends = [(1, 0), (2, 0), (3, 0), (0, 1), (0, 2), (0, 3), (1, 1), (-1, -1)]
    for dlon, dlat in friends:
        pl.semaphore_signal(
            barrier, inc=1, device_id=at(dlon, dlat), device_id_type=pl.DeviceIdType.MESH
        )

    pk[:, :, :, 0:C] = x_ref[...]
    pk[:, :, :, C : 2 * C] = g_ref[...]
    sg[0:3, 0] = pk[3:6, 1]
    pl.semaphore_wait(barrier, len(friends))
    halo = [
        remote(pk.at[pl.ds(3, 3), 0], sg.at[pl.ds(0, 3), 1], halo_send.at[0], halo_recv.at[0], at(-1, 0)),
        remote(pk.at[pl.ds(0, 3), 0], sg.at[pl.ds(3, 3), 1], halo_send.at[2], halo_recv.at[2], at(-1, -1)),
        remote(pk.at[pl.ds(0, 3), 1], sg.at[pl.ds(3, 3), 0], halo_send.at[1], halo_recv.at[1], at(0, -1)),
    ]
    for copy in halo:
        copy.start()

    tabx[...] = jnp.zeros_like(tabx)
    for p in range(12):
        tabx[:, 32 * p : 32 * p + 23] = tab_ref[pl.ds(p, 288, stride=12), :]
    table = tabx[...]
    top = table.astype(bf16)
    rest = table - top.astype(f32)
    mid = rest.astype(bf16)
    low_part = (rest - mid.astype(f32)).astype(bf16)
    spread = gm_ref[...]
    spreaded = dot_nn(top, spread) + dot_nn(mid, spread) + dot_nn(low_part, spread)
    for i in range(4):
        tp[i] = spreaded[72 * i : 72 * i + 72]

    def expand(i, carry):
        for h in range(HEADS):
            for c in range(12):
                bias[i, h, 12 * c : 12 * c + 12, :] = tp[
                    i, 12 * h : 12 * h + 12, 12 * (11 - c) : 12 * (11 - c) + WIN
                ]
        return carry

    lax.fori_loop(0, 4, expand, 0)
    for n in range(4):
        wl[n] = jnp.zeros((16, 768), bf16)
    spot = lax.broadcasted_iota(jnp.int32, (1, 576), 1)
    keep = jnp.where((spot >= 288) & (lat == nt - 1), 0.0, 1.0).astype(bf16)
    pm = pm_ref[...] * keep
    rows = lax.broadcasted_iota(jnp.int32, (WIN, WIN), 0)
    cols = lax.broadcasted_iota(jnp.int32, (WIN, WIN), 1)
    same = rows == cols
    for copy in halo:
        copy.wait()

    both = dot_nn(pm, sg[...].reshape(576, 2 * C)).astype(bf16)
    xs = both[:, :C]
    gs_all = both[:, C:]
    xa[...] = xs
    ga[...] = gs_all
    qkv_all = dot_nn(xs, wq_ref[...]).astype(bf16)
    gatt_all = dot_nt(gs_all, wp_ref[...]).astype(bf16)
    for i in range(4):
        qa[i] = qkv_all[WIN * i : WIN * i + WIN]
        ca[i] = gatt_all[WIN * i : WIN * i + WIN]
    temper = HEAD_DIM ** (-0.5)
    lane = lax.broadcasted_iota(jnp.int32, (WIN, 8), 1)

    def bias_copy(s):
        w = lax.rem(lon + 1 + s, nl)
        return remote(bs.at[w], br.at[s], bsum_send.at[s], bsum_recv.at[s], at(1 + s, 0))

    def window(s, carry):
        w = lax.rem(lon + 1 + s, nl)
        code = ids_ref[w]
        usable = code >= 4
        region = jnp.where(usable, code - 4, code)
        hot = jnp.where(region == lane, 1.0, 0.0).astype(bf16)
        keyed = jnp.where(usable & (region == lane), 1.0, 0.0).astype(bf16)
        allowed = (dot_nt(hot, keyed) > 0.5) | same
        fold[...] = jnp.zeros_like(fold)
        for h in range(HEADS):
            lo = HEAD_DIM * h
            q = qa[w, :, lo : lo + 32]
            k = qa[w, :, C + lo : C + lo + 32]
            v = qa[w, :, 2 * C + lo : 2 * C + lo + 32]
            go = ca[w, :, lo : lo + 32]
            scores = dot_nt(q, k) * temper + bias[w, h]
            scores = jnp.where(allowed, scores, masked_score)
            power = jnp.exp(scores - jnp.max(scores, axis=-1, keepdims=True))
            probs = power * (1.0 / jnp.sum(power, axis=-1, keepdims=True))
            low = probs.astype(bf16)
            aa[w, :, lo : lo + 32] = dot_nn(low, v).astype(bf16)
            gp = dot_nt(go, v)
            gs = probs * (gp - jnp.sum(probs * gp, axis=-1, keepdims=True))
            dsr[h] = gs
            scaled = (gs * temper).astype(bf16)
            gr[w, :, lo : lo + 32] = dot_nn(scaled, k).astype(bf16)
            gr[w, :, C + lo : C + lo + 32] = dot_tn(scaled, q).astype(bf16)
            gr[w, :, 2 * C + lo : 2 * C + lo + 32] = dot_tn(low, go).astype(bf16)
            for c in range(12):
                off = 12 * (11 - c)
                fold[12 * h : 12 * h + 12, off : off + WIN] += dsr[h, 12 * c : 12 * c + 12, :]
        bs[w] = dot_nn(fold[...].astype(bf16), gmt_ref[...]).astype(bf16)

        @pl.when(s < 3)
        def _():
            bias_copy(s).start()

        return carry

    lax.fori_loop(0, 4, window, 0)

    grads = gr[...].reshape(576, 576)
    dw[:, :576] = dot_tn(xa[...], grads)
    dw[:, 576:] = dot_tn(aa[...].reshape(576, C), ga[...])
    for n in range(4):
        ws[n % 2, n // 2] = dw[48 * n : 48 * n + 48, :].astype(bf16)
    mate = {"lat": lat + 1 - 2 * core}
    first = remote(ws.at[1 - core], wr1, pair_send.at[0], pair_recv.at[0], mate)
    first.start()

    back = dot_nt(grads, wq_ref[...]).astype(bf16)
    hs[...] = dot_nn(pt_ref[...], back).astype(bf16).reshape(6, 2, PAD, C)

    first.wait()
    w2[...] = (ws[core].astype(f32) + wr1[...].astype(f32)).astype(bf16)
    across = {"lat": lax.rem(lat + 2, nt)}
    second = remote(w2.at[1 - far_y], wr2, pair_send.at[1], pair_recv.at[1], across)
    second.start()
    home = [
        remote(hs.at[pl.ds(0, 3), 1], og.at[pl.ds(3, 3), 0], back_send.at[0], back_recv.at[0], at(1, 0)),
        remote(hs.at[pl.ds(3, 3), 1], og.at[pl.ds(0, 3), 0], back_send.at[2], back_recv.at[2], at(1, 1)),
        remote(hs.at[pl.ds(3, 3), 0], og.at[pl.ds(0, 3), 1], back_send.at[1], back_recv.at[1], at(0, 1)),
    ]

    for s in range(3):
        bias_copy(s).wait()
    total = bs[lon].astype(f32)
    for s in range(3):
        total = total + br[s].astype(f32)
    bg[...] = total.astype(bf16)

    second.wait()
    part_sum = w2[far_y].astype(f32) + wr2[...].astype(f32)
    dw[0:48, :] = part_sum
    for n in range(4):
        wl[n, 0:12, :] = dw[12 * n : 12 * n + 12, :].astype(bf16)
    wb = []
    for d in range(1, 4):
        to = lax.rem(lon + d, nl)
        wb.append(
            remote(wl.at[to], wm.at[d - 1], wb_send.at[d - 1], wb_recv.at[d - 1], at(d, 0))
        )
    for copy in wb:
        copy.start()
    for copy in home:
        copy.start()
    ball = [
        remote(bg, bo.at[lon], ball_send.at[d - 1], ball_recv.at[d - 1], at(d, 0))
        for d in range(1, 4)
    ]

    og[3:6, 1] = hs[0:3, 0]
    bo[lon] = bg[...]
    for copy in wb:
        copy.wait()
    mine = wl[lon].astype(f32)
    for d in range(3):
        mine = mine + wm[d].astype(f32)
    wf[...] = mine.astype(bf16)
    wo[core, far_y, lon] = wf[...]
    wc = [
        remote(wf, wo.at[core, far_y, lon], wc_send.at[d - 1], wc_recv.at[d - 1], at(d, 0))
        for d in range(1, 4)
    ]
    for copy in wc:
        copy.start()
    for copy in ball:
        copy.start()
    for copy in wc:
        copy.wait()
    own = wo.at[core, far_y]
    third = remote(own, own, pair_send.at[2], pair_recv.at[2], across)
    third.start()

    for copy in home:
        copy.wait()
    fill = jnp.where(lat == 0, 0.0, 1.0).astype(bf16)
    out_x[0:3] = og[0:3] * fill
    out_x[3:6] = og[3:6]

    third.wait()
    half = wo.at[core]
    fourth = remote(half, half, pair_send.at[3], pair_recv.at[3], mate)
    fourth.start()

    for copy in ball:
        copy.wait()
    for i in range(4):
        piece = bo[i].astype(f32)
        for p in range(12):
            out_b[pl.ds(864 * i + p, 72, stride=12), :] = piece[0:72, 32 * p : 32 * p + 23]

    fourth.wait()
    for n in range(16):
        piece = wo[(n // 4) % 2, n // 8, n % 4].astype(f32) * factor
        out_w[12 * n : 12 * n + 12, :] = piece[0:12, :576]
        out_p[12 * n : 12 * n + 12, :] = piece[0:12, 576:]


def fused_body(attn_input, out_grad, w_qkv, w_proj, bias_table, mask_ids, valid_rows):
    f32, bf16 = jnp.float32, jnp.bfloat16
    levels, lat_rows, lon_cols, _ = attn_input.shape
    anchor = jnp.arange(lat_rows, dtype=jnp.int32) + lax.axis_index("lat") * lat_rows + WLAT // 2
    usable = (anchor < valid_rows[0])[None, :, None]
    codes = jnp.where(usable, mask_ids + 4, mask_ids)
    codes = codes.reshape(4, 2, 6, 12).transpose(0, 3, 1, 2).reshape(4, WIN, 1)
    table = bias_table.transpose(0, 1, 2, 3, 5, 6, 4, 7).reshape(3456, 23)

    def turned(field):
        return field.transpose(1, 2, 0, 3).reshape(6, 2, PAD, C)

    order = place_map()
    spread = bias_map()
    maps = [jnp.asarray(m, bf16) for m in (order, order.T, spread, spread.T)]
    cells = levels * lat_rows * lax.axis_size("lat") * lon_cols * lax.axis_size("lon")
    vm = pltpu.VMEM
    sem = pltpu.SemaphoreType.DMA((3,))
    four = pltpu.SemaphoreType.DMA((4,))
    scratch = [
        vm((6, 2, PAD, 2 * C), bf16),
        vm((6, 2, PAD, 2 * C), bf16),
        vm((6, 2, PAD, C), bf16),
        vm((6, 2, PAD, C), bf16),
        vm((4, HEADS, WIN, WIN), f32),
        vm((288, 384), f32),
        vm((4, 72, 384), f32),
        vm((80, 384), f32),
        vm((HEADS, WIN, WIN), f32),
        vm((576, C), bf16),
        vm((576, C), bf16),
        vm((4, WIN, C), bf16),
        vm((4, WIN, 3 * C), bf16),
        vm((4, WIN, 3 * C), bf16),
        vm((4, WIN, C), bf16),
        vm((C, 768), f32),
        vm((2, 2, 48, 768), bf16),
        vm((2, 48, 768), bf16),
        vm((2, 48, 768), bf16),
        vm((48, 768), bf16),
        vm((4, 16, 768), bf16),
        vm((3, 16, 768), bf16),
        vm((16, 768), bf16),
        vm((2, 2, 4, 16, 768), bf16),
        vm((4, 80, 384), bf16),
        vm((3, 80, 384), bf16),
        vm((80, 384), bf16),
        vm((4, 80, 384), bf16),
    ] + [sem] * 12 + [four] * 2
    whole = pl.BlockSpec(memory_space=pltpu.VMEM)
    grad_input, grad_qkv, grad_proj, folded = pl.pallas_call(
        functools.partial(kernel, cells ** (-0.5)),
        out_shape=(
            jax.ShapeDtypeStruct((6, 2, PAD, C), bf16),
            jax.ShapeDtypeStruct((C, 3 * C), f32),
            jax.ShapeDtypeStruct((C, C), f32),
            jax.ShapeDtypeStruct((3456, 23), f32),
        ),
        in_specs=[whole] * 10,
        out_specs=[whole] * 4,
        scratch_shapes=scratch,
        compiler_params=pltpu.CompilerParams(
            collective_id=0, has_side_effects=True, vmem_limit_bytes=48 * 1024 * 1024
        ),
    )(turned(attn_input), turned(out_grad), w_qkv, w_proj, table, codes, *maps)
    grad_input = grad_input.reshape(6, 12, 8, C).transpose(2, 0, 1, 3)
    folded = folded.reshape(4, 1, 6, 2, 6, 6, 2, 23)
    return grad_input, grad_qkv, grad_proj, folded.transpose(0, 1, 2, 3, 6, 4, 5, 7)


def fitting_body(attn_input, *others):
    tuned = (
        lax.axis_size("lon") == 4
        and lax.axis_size("lat") == 4
        and attn_input.shape == (8, 6, 12, C)
    )
    return (fused_body if tuned else body)(attn_input, *others)


PAD = 48


def solution(mesh):
    placed = (
        P("batch", "lat", "lon", None),
        P("batch", "lat", "lon", None),
        P(),
        P(),
        P(None, "lat", None, None, None, None, None, None),
        P("batch", "lat", "lon"),
        P("batch"),
    )
    return jax.shard_map(
        fitting_body,
        mesh=mesh,
        in_specs=placed,
        out_specs=(
            P("batch", "lat", "lon", None),
            P("batch", None),
            P("batch", None),
            P("batch", "lat", None, None, None, None, None, None),
        ),
        check_vma=False,
    )
```

```python
import functools

import jax
import jax.numpy as jnp
import numpy as np
from jax import lax
from jax.experimental import pallas as pl
from jax.experimental.pallas import tpu as pltpu
from jax.sharding import PartitionSpec as P

C = 192
HEADS = 6
HEAD_DIM = 32
WZ = 2
WLAT = 6
WLON = 12
WIN = 144


masked_score = -1000000000.0


def from_behind(shard, axis, by):
    devices = lax.axis_size(axis)
    return lax.ppermute(shard, axis, [(i, (i + by) % devices) for i in range(devices)])


def shifted_2(shard, axis, by):
    devices = lax.axis_size(axis)
    pairs = [(i, i + by) for i in range(devices) if 0 <= i + by < devices]
    return lax.ppermute(shard, axis, pairs)


def lon_table():
    column = jnp.arange(WLON, dtype=jnp.int32)
    offset = jnp.arange(2 * WLON - 1, dtype=jnp.int32)
    return (
        column[:, None, None] - column[None, :, None] + (WLON - 1) == offset[None, None, :]
    ).astype(jnp.float32)


def expand_bias(folded):
    expanded = jnp.einsum(
        "...hxyuvr,abr->...hxuayvb", folded, lon_table(), precision=lax.Precision.HIGHEST
    )
    return expanded.reshape(expanded.shape[:-7] + (HEADS, WIN, WIN))


def fold_bias(grads):
    divided = grads.reshape(grads.shape[:-3] + (HEADS, WZ, WLAT, WLON, WZ, WLAT, WLON))
    return jnp.einsum(
        "...hxuayvb,abr->...hxyuvr", divided, lon_table(), precision=lax.Precision.HIGHEST
    )


def to_windows(grid_field):
    levels, lat_rows, lon_cols = grid_field.shape[:3]
    trailing = grid_field.shape[3:]
    divided = grid_field.reshape(
        (levels // WZ, WZ, lat_rows // WLAT, WLAT, lon_cols // WLON, WLON) + trailing
    )
    arrangement = (0, 2, 4, 1, 3, 5) + tuple(range(6, 6 + len(trailing)))
    return divided.transpose(arrangement).reshape(
        (levels // WZ, lat_rows // WLAT, lon_cols // WLON, WIN) + trailing
    )


def from_windows(windows, levels, lat_rows, lon_cols):
    trailing = windows.shape[4:]
    divided = windows.reshape(
        (levels // WZ, lat_rows // WLAT, lon_cols // WLON, WZ, WLAT, WLON) + trailing
    )
    arrangement = (0, 3, 1, 4, 2, 5) + tuple(range(6, 6 + len(trailing)))
    return divided.transpose(arrangement).reshape((levels, lat_rows, lon_cols) + trailing)


def outer_part(grid_field, cut_width, axis, leading):
    length = grid_field.shape[axis]
    if leading:
        return lax.slice_in_dim(grid_field, 0, cut_width, axis=axis)
    return lax.slice_in_dim(grid_field, length - cut_width, length, axis=axis)


def inner_part(grid_field, cut_width, axis, leading):
    length = grid_field.shape[axis]
    if leading:
        return lax.slice_in_dim(grid_field, cut_width, length, axis=axis)
    return lax.slice_in_dim(grid_field, 0, length - cut_width, axis=axis)


def attach(kept, arrived, axis, leading):
    if leading:
        return jnp.concatenate([kept, arrived], axis=axis)
    return jnp.concatenate([arrived, kept], axis=axis)


def displace(fields, heading):
    leading = heading < 0
    fields = [jnp.roll(grid_field, heading * (WZ // 2), axis=0) for grid_field in fields]
    border = jnp.stack([outer_part(grid_field, WLON // 2, 2, leading) for grid_field in fields])
    arrived = from_behind(border, "lon", heading)
    fields = [
        attach(inner_part(grid_field, WLON // 2, 2, leading), arrived[number], 2, leading)
        for number, grid_field in enumerate(fields)
    ]
    border = jnp.stack([outer_part(grid_field, WLAT // 2, 1, leading) for grid_field in fields])
    arrived = shifted_2(border, "lat", heading)
    return [
        attach(inner_part(grid_field, WLAT // 2, 1, leading), arrived[number], 1, leading)
        for number, grid_field in enumerate(fields)
    ]


def window_backward(shifted, grads_y, allowed, bias, w_qkv, w_proj):
    groups = shifted.shape[0]
    flattened = shifted.reshape(groups * WIN, C)
    projected = jnp.dot(flattened, w_qkv, preferred_element_type=jnp.float32).astype(jnp.bfloat16)
    projected = projected.reshape(groups, WIN, 3, HEADS, HEAD_DIM)
    query_rows = projected[:, :, 0]
    key_rows = projected[:, :, 1]
    value_rows = projected[:, :, 2]
    temper = HEAD_DIM ** (-0.5)
    scores = (
        jnp.einsum("gnhd,gmhd->ghnm", query_rows, key_rows, preferred_element_type=jnp.float32)
        * temper
        + bias
    )
    scores = jnp.where(allowed[:, None], scores, masked_score)
    exponent = jnp.exp(scores - jnp.max(scores, axis=-1, keepdims=True))
    attn_probs = exponent / jnp.sum(exponent, axis=-1, keepdims=True)
    probs_low = attn_probs.astype(jnp.bfloat16)
    attended = jnp.einsum(
        "ghnm,gmhd->gnhd", probs_low, value_rows, preferred_element_type=jnp.float32
    )
    attended = attended.astype(jnp.bfloat16).reshape(groups * WIN, C)
    upstream = grads_y.reshape(groups * WIN, C)
    grad_proj = jnp.einsum("tc,te->ce", attended, upstream, preferred_element_type=jnp.float32)
    grad_att = jnp.einsum("te,ce->tc", upstream, w_proj, preferred_element_type=jnp.float32)
    grad_att = grad_att.astype(jnp.bfloat16).reshape(groups, WIN, HEADS, HEAD_DIM)
    grad_prob = jnp.einsum(
        "gnhd,gmhd->ghnm", grad_att, value_rows, preferred_element_type=jnp.float32
    )
    grad_score = attn_probs * (grad_prob - jnp.sum(attn_probs * grad_prob, axis=-1, keepdims=True))
    scaled = (grad_score * temper).astype(jnp.bfloat16)
    grad_query = jnp.einsum("ghnm,gmhd->gnhd", scaled, key_rows, preferred_element_type=jnp.float32)
    grad_key = jnp.einsum("ghnm,gnhd->gmhd", scaled, query_rows, preferred_element_type=jnp.float32)
    grad_value = jnp.einsum(
        "ghnm,gnhd->gmhd", probs_low, grad_att, preferred_element_type=jnp.float32
    )
    grad_rows = (
        jnp.stack([grad_query, grad_key, grad_value], axis=2)
        .astype(jnp.bfloat16)
        .reshape(groups * WIN, 3 * C)
    )
    weight_qkv = jnp.einsum("tc,te->ce", flattened, grad_rows, preferred_element_type=jnp.float32)
    grad_shifted = jnp.einsum(
        "te,ce->tc", grad_rows, w_qkv, preferred_element_type=jnp.float32
    ).astype(jnp.bfloat16)
    return (grad_shifted.reshape(groups, WIN, C), weight_qkv, grad_proj, grad_score)


def body(attn_input, out_grad, w_qkv, w_proj, bias_table, mask_ids, valid_rows):
    levels, lat_rows, lon_cols, channels = attn_input.shape
    moved_input, moved_grad = displace([attn_input, out_grad], -1)
    shifted = to_windows(moved_input)
    grads_y = to_windows(moved_grad)
    anchor = jnp.arange(lat_rows, dtype=jnp.int32) + lax.axis_index("lat") * lat_rows + WLAT // 2
    usable = jnp.broadcast_to((anchor < valid_rows[0])[None, :, None], (levels, lat_rows, lon_cols))
    regions = to_windows(mask_ids)
    usable_win = to_windows(usable)
    allowed = (regions[..., :, None] == regions[..., None, :]) & usable_win[..., None, :]
    allowed = allowed | jnp.eye(WIN, dtype=bool)
    bias_full = expand_bias(bias_table)
    level_wins, lat_wins, lon_wins = shifted.shape[:3]

    def regroup(windows):
        rotated = jnp.moveaxis(windows, 1, 0)
        return rotated.reshape((lat_wins, level_wins * lon_wins) + windows.shape[3:])

    def one_band(pieces):
        band_input, band_grads, band_mask, band_bias = pieces
        expanded = band_bias[:, None]
        expanded = expanded.reshape(level_wins * lon_wins, HEADS, WIN, WIN)
        grad_in, weight_qkv, weight_proj, grad_score = window_backward(
            band_input, band_grads, band_mask, expanded, w_qkv, w_proj
        )
        folded = fold_bias(
            jnp.sum(grad_score.reshape(level_wins, lon_wins, HEADS, WIN, WIN), axis=1)
        )
        return (grad_in, weight_qkv, weight_proj, folded)

    grad_in, weight_qkv, weight_proj, folded = lax.map(
        one_band,
        (regroup(shifted), regroup(grads_y), regroup(allowed), jnp.moveaxis(bias_full, 1, 0)),
    )
    grad_in = jnp.moveaxis(grad_in.reshape((lat_wins, level_wins, lon_wins, WIN, channels)), 0, 1)
    grad_input = displace([from_windows(grad_in, levels, lat_rows, lon_cols)], 1)[0]
    local_qkv = jnp.sum(weight_qkv, axis=0)
    local_proj = jnp.sum(weight_proj, axis=0)
    local_table = jnp.moveaxis(folded, 0, 1)
    total_qkv, total_proj = lax.psum((local_qkv, local_proj), ("lon", "lat"))
    grad_bias = lax.psum(local_table, "lon")
    cells = levels * lat_rows * lax.axis_size("lat") * lon_cols * lax.axis_size("lon")
    factor = cells ** (-0.5)
    return (grad_input, total_qkv * factor, total_proj * factor, grad_bias)

def place_map():
    order = np.zeros((576, 576), np.float32)
    for i in range(4):
        for c in range(12):
            for a in range(2):
                for b in range(6):
                    order[i * WIN + c * 12 + a * 6 + b, b * 96 + c * 8 + (2 * i + a + 1) % 8] = 1.0
    return order


def bias_map():
    spread = np.zeros((384, 384), np.float32)
    for a in range(2):
        for b in range(6):
            for d in range(23):
                spread[(2 * b + a) * 32 + d, (22 - d) * 12 + a * 6 + b] = 1.0
    return spread


def dot_nn(a, b):
    return lax.dot_general(a, b, (((1,), (0,)), ((), ())), preferred_element_type=jnp.float32)


def dot_nt(a, b):
    return lax.dot_general(a, b, (((1,), (1,)), ((), ())), preferred_element_type=jnp.float32)


def dot_tn(a, b):
    return lax.dot_general(a, b, (((0,), (0,)), ((), ())), preferred_element_type=jnp.float32)


def kernel(
    x_hbm, g_hbm, tab_hbm, gm_hbm, pm_hbm, wq_hbm, wp_hbm, gmt_hbm, pt_hbm, ids_ref,
    out_x, out_w, out_b,
    x_ref, g_ref, tab_ref, gm_ref, pm_ref, wq_ref, wp_ref, gmt_ref, pt_ref, fetch_sem,
    pk, sg, hs, og, bias, tabx, tp, fold, dsr, xa, ga, aa, gr, qa, ca, dw,
    ws, wr1, w2, wr2, wl, wm, wf, wo, bs, br, bg, bo,
    halo_send, halo_recv, back_send, back_recv, bsum_send, bsum_recv, ball_send, ball_recv,
    wb_send, wb_recv, wc_send, wc_recv, pair_send, pair_recv,
):
    f32, bf16 = jnp.float32, jnp.bfloat16
    lon, lat = lax.axis_index("lon"), lax.axis_index("lat")
    nl, nt = 4, 4
    core, far_y = lax.rem(lat, 2), lat // 2

    def at(dlon, dlat):
        return {"lon": lax.rem(lon + dlon + nl, nl), "lat": lax.rem(lat + dlat + nt, nt)}

    def remote(src, dst, send, recv, where):
        return pltpu.make_async_remote_copy(
            src_ref=src, dst_ref=dst, send_sem=send, recv_sem=recv,
            device_id=where, device_id_type=pl.DeviceIdType.MESH,
        )

    fetches = [
        pltpu.make_async_copy(src, dst, fetch_sem.at[n])
        for n, (src, dst) in enumerate(
            (
                (x_hbm, x_ref), (g_hbm, g_ref), (tab_hbm, tab_ref), (gm_hbm, gm_ref),
                (pm_hbm, pm_ref), (wq_hbm, wq_ref), (wp_hbm, wp_ref), (gmt_hbm, gmt_ref),
                (pt_hbm, pt_ref),
            )
        )
    ]
    for fetch in fetches:
        fetch.start()
    barrier = pltpu.get_barrier_semaphore()
    friends = [(1, 0), (2, 0), (3, 0), (0, 1), (0, 2), (0, 3), (1, 1), (-1, -1)]
    for dlon, dlat in friends:
        pl.semaphore_signal(
            barrier, inc=1, device_id=at(dlon, dlat), device_id_type=pl.DeviceIdType.MESH
        )

    fetches[0].wait()
    fetches[1].wait()
    pk[:, :, :, 0:C] = x_ref[...]
    pk[:, :, :, C : 2 * C] = g_ref[...]
    sg[0:3, 0] = pk[3:6, 1]
    pl.semaphore_wait(barrier, len(friends))
    halo = [
        remote(pk.at[pl.ds(3, 3), 0], sg.at[pl.ds(0, 3), 1], halo_send.at[0], halo_recv.at[0], at(-1, 0)),
        remote(pk.at[pl.ds(0, 3), 0], sg.at[pl.ds(3, 3), 1], halo_send.at[2], halo_recv.at[2], at(-1, -1)),
        remote(pk.at[pl.ds(0, 3), 1], sg.at[pl.ds(3, 3), 0], halo_send.at[1], halo_recv.at[1], at(0, -1)),
    ]
    for copy in halo:
        copy.start()

    tabx[...] = jnp.zeros_like(tabx)
    for fetch in fetches[2:]:
        fetch.wait()
    for p in range(12):
        tabx[:, 32 * p : 32 * p + 23] = tab_ref[pl.ds(p, 288, stride=12), :]
    table = tabx[...]
    top = table.astype(bf16)
    rest = table - top.astype(f32)
    mid = rest.astype(bf16)
    low_part = (rest - mid.astype(f32)).astype(bf16)
    spread = gm_ref[...]
    spreaded = dot_nn(top, spread) + dot_nn(mid, spread) + dot_nn(low_part, spread)
    for i in range(4):
        tp[i] = spreaded[72 * i : 72 * i + 72]

    def expand(i, carry):
        for h in range(HEADS):
            for c in range(12):
                bias[i, h, 12 * c : 12 * c + 12, :] = tp[
                    i, 12 * h : 12 * h + 12, 12 * (11 - c) : 12 * (11 - c) + WIN
                ]
        return carry

    lax.fori_loop(0, 4, expand, 0)
    for n in range(4):
        wl[n] = jnp.zeros((16, 768), bf16)
    spot = lax.broadcasted_iota(jnp.int32, (1, 576), 1)
    keep = jnp.where((spot >= 288) & (lat == nt - 1), 0.0, 1.0).astype(bf16)
    pm = pm_ref[...] * keep
    rows = lax.broadcasted_iota(jnp.int32, (WIN, WIN), 0)
    cols = lax.broadcasted_iota(jnp.int32, (WIN, WIN), 1)
    same = rows == cols
    for copy in halo:
        copy.wait()

    both = dot_nn(pm, sg[...].reshape(576, 2 * C)).astype(bf16)
    xs = both[:, :C]
    gs_all = both[:, C:]
    xa[...] = xs
    ga[...] = gs_all
    qkv_all = dot_nn(xs, wq_ref[...]).astype(bf16)
    gatt_all = dot_nt(gs_all, wp_ref[...]).astype(bf16)
    for i in range(4):
        qa[i] = qkv_all[WIN * i : WIN * i + WIN]
        ca[i] = gatt_all[WIN * i : WIN * i + WIN]
    temper = HEAD_DIM ** (-0.5)
    lane = lax.broadcasted_iota(jnp.int32, (WIN, 8), 1)

    def bias_copy(s):
        w = lax.rem(lon + 1 + s, nl)
        return remote(bs.at[w], br.at[s], bsum_send.at[s], bsum_recv.at[s], at(1 + s, 0))

    def window(s, carry):
        w = lax.rem(lon + 1 + s, nl)
        code = ids_ref[w]
        usable = code >= 4
        region = jnp.where(usable, code - 4, code)
        hot = jnp.where(region == lane, 1.0, 0.0).astype(bf16)
        keyed = jnp.where(usable & (region == lane), 1.0, 0.0).astype(bf16)
        allowed = (dot_nt(hot, keyed) > 0.5) | same
        fold[...] = jnp.zeros_like(fold)
        held = []
        for h in range(HEADS):
            lo = HEAD_DIM * h
            q = qa[w, :, lo : lo + 32]
            k = qa[w, :, C + lo : C + lo + 32]
            v = qa[w, :, 2 * C + lo : 2 * C + lo + 32]
            go = ca[w, :, lo : lo + 32]
            held.append((q, k, v, go, dot_nt(q, k), dot_nt(go, v)))
        ready = []
        for h, (q, k, v, go, raw, gp) in enumerate(held):
            scores = jnp.where(allowed, raw * temper + bias[w, h], masked_score)
            power = jnp.exp(scores - jnp.max(scores, axis=-1, keepdims=True))
            probs = power * (1.0 / jnp.sum(power, axis=-1, keepdims=True))
            gs = probs * (gp - jnp.sum(probs * gp, axis=-1, keepdims=True))
            dsr[h] = gs
            ready.append((probs.astype(bf16), (gs * temper).astype(bf16)))
        for h, (low, scaled) in enumerate(ready):
            q, k, v, go = held[h][:4]
            lo = HEAD_DIM * h
            aa[w, :, lo : lo + 32] = dot_nn(low, v).astype(bf16)
            gr[w, :, lo : lo + 32] = dot_nn(scaled, k).astype(bf16)
            gr[w, :, C + lo : C + lo + 32] = dot_tn(scaled, q).astype(bf16)
            gr[w, :, 2 * C + lo : 2 * C + lo + 32] = dot_tn(low, go).astype(bf16)
            for c in range(12):
                off = 12 * (11 - c)
                fold[12 * h : 12 * h + 12, off : off + WIN] += dsr[h, 12 * c : 12 * c + 12, :]
        bs[w] = dot_nn(fold[...].astype(bf16), gmt_ref[...]).astype(bf16)

        @pl.when(s < 3)
        def _():
            bias_copy(s).start()

        return carry

    lax.fori_loop(0, 4, window, 0)

    grads = gr[...].reshape(576, 576)
    dw[:, :576] = dot_tn(xa[...], grads)
    dw[:, 576:] = dot_tn(aa[...].reshape(576, C), ga[...])
    for n in range(4):
        ws[n % 2, n // 2] = dw[48 * n : 48 * n + 48, :].astype(bf16)
    mate = {"lat": lat + 1 - 2 * core}
    first = remote(ws.at[1 - core], wr1, pair_send.at[0], pair_recv.at[0], mate)
    first.start()

    back = dot_nt(grads, wq_ref[...]).astype(bf16)
    hs[...] = dot_nn(pt_ref[...], back).astype(bf16).reshape(6, 2, PAD, C)

    first.wait()
    w2[...] = (ws[core].astype(f32) + wr1[...].astype(f32)).astype(bf16)
    across = {"lat": lax.rem(lat + 2, nt)}
    second = remote(w2.at[1 - far_y], wr2, pair_send.at[1], pair_recv.at[1], across)
    second.start()
    home = [
        remote(hs.at[pl.ds(0, 3), 1], og.at[pl.ds(3, 3), 0], back_send.at[0], back_recv.at[0], at(1, 0)),
        remote(hs.at[pl.ds(3, 3), 1], og.at[pl.ds(0, 3), 0], back_send.at[2], back_recv.at[2], at(1, 1)),
        remote(hs.at[pl.ds(3, 3), 0], og.at[pl.ds(0, 3), 1], back_send.at[1], back_recv.at[1], at(0, 1)),
    ]

    for copy in home:
        copy.start()
    for s in range(3):
        bias_copy(s).wait()
    total = bs[lon].astype(f32)
    for s in range(3):
        total = total + br[s].astype(f32)
    bg[...] = total.astype(bf16)

    second.wait()
    part_sum = w2[far_y].astype(f32) + wr2[...].astype(f32)
    dw[0:48, :] = part_sum
    for n in range(4):
        wl[n, 0:12, :] = dw[12 * n : 12 * n + 12, :].astype(bf16)
    wb = []
    for d in range(1, 4):
        to = lax.rem(lon + d, nl)
        wb.append(
            remote(wl.at[to], wm.at[d - 1], wb_send.at[d - 1], wb_recv.at[d - 1], at(d, 0))
        )
    for copy in wb:
        copy.start()
    ball = [
        remote(bg, bo.at[lon], ball_send.at[d - 1], ball_recv.at[d - 1], at(d, 0))
        for d in range(1, 4)
    ]

    og[3:6, 1] = hs[0:3, 0]
    bo[lon] = bg[...]
    for copy in wb:
        copy.wait()
    mine = wl[lon].astype(f32)
    for d in range(3):
        mine = mine + wm[d].astype(f32)
    wf[...] = mine.astype(bf16)
    wo[core, far_y, lon] = wf[...]
    wc = [
        remote(wf, wo.at[core, far_y, lon], wc_send.at[d - 1], wc_recv.at[d - 1], at(d, 0))
        for d in range(1, 4)
    ]
    for copy in wc:
        copy.start()
    for copy in ball:
        copy.start()
    for copy in wc:
        copy.wait()
    own = wo.at[core, far_y]
    third = remote(own, own, pair_send.at[2], pair_recv.at[2], across)
    third.start()

    for copy in home:
        copy.wait()
    fill = jnp.where(lat == 0, 0.0, 1.0).astype(bf16)
    out_x[0:3] = og[0:3] * fill
    out_x[3:6] = og[3:6]

    third.wait()
    half = wo.at[core]
    fourth = remote(half, half, pair_send.at[3], pair_recv.at[3], mate)
    fourth.start()

    for copy in ball:
        copy.wait()
    out_b[...] = bo[...]
    fourth.wait()
    out_w[...] = wo[...]


def finish(factor, og_hbm, wo_hbm, bo_hbm, out_x, out_w, out_p, out_b, wo, bo, sems):
    f32 = jnp.float32
    fetches = [
        pltpu.make_async_copy(src, dst, sems.at[n])
        for n, (src, dst) in enumerate(((bo_hbm, bo), (wo_hbm, wo), (og_hbm, out_x)))
    ]
    for fetch in fetches:
        fetch.start()
    fetches[0].wait()
    for i in range(4):
        piece = bo[i].astype(f32)
        for p in range(12):
            out_b[pl.ds(864 * i + p, 72, stride=12), :] = piece[0:72, 32 * p : 32 * p + 23]
    fetches[1].wait()
    for n in range(16):
        piece = wo[(n // 4) % 2, n // 8, n % 4].astype(f32) * factor
        out_w[12 * n : 12 * n + 12, :] = piece[0:12, :576]
        out_p[12 * n : 12 * n + 12, :] = piece[0:12, 576:]
    fetches[2].wait()


def fused_body(attn_input, out_grad, w_qkv, w_proj, bias_table, mask_ids, valid_rows):
    f32, bf16 = jnp.float32, jnp.bfloat16
    levels, lat_rows, lon_cols, _ = attn_input.shape
    anchor = jnp.arange(lat_rows, dtype=jnp.int32) + lax.axis_index("lat") * lat_rows + WLAT // 2
    usable = (anchor < valid_rows[0])[None, :, None]
    codes = jnp.where(usable, mask_ids + 4, mask_ids)
    codes = codes.reshape(4, 2, 6, 12).transpose(0, 3, 1, 2).reshape(4, WIN, 1)
    table = bias_table.transpose(0, 1, 2, 3, 5, 6, 4, 7).reshape(3456, 23)

    def turned(field):
        return field.transpose(1, 2, 0, 3).reshape(6, 2, PAD, C)

    order = place_map()
    spread = bias_map()
    maps = [jnp.asarray(m, bf16) for m in (order, order.T, spread, spread.T)]
    cells = levels * lat_rows * lax.axis_size("lat") * lon_cols * lax.axis_size("lon")
    vm = pltpu.VMEM
    sem = pltpu.SemaphoreType.DMA((3,))
    four = pltpu.SemaphoreType.DMA((4,))
    scratch = [
        vm((6, 2, PAD, C), bf16),
        vm((6, 2, PAD, C), bf16),
        vm((3456, 23), f32),
        vm((384, 384), bf16),
        vm((576, 576), bf16),
        vm((C, 3 * C), bf16),
        vm((C, C), bf16),
        vm((384, 384), bf16),
        vm((576, 576), bf16),
        pltpu.SemaphoreType.DMA((9,)),
        vm((6, 2, PAD, 2 * C), bf16),
        vm((6, 2, PAD, 2 * C), bf16),
        vm((6, 2, PAD, C), bf16),
        vm((6, 2, PAD, C), bf16),
        vm((4, HEADS, WIN, WIN), f32),
        vm((288, 384), f32),
        vm((4, 72, 384), f32),
        vm((80, 384), f32),
        vm((HEADS, WIN, WIN), f32),
        vm((576, C), bf16),
        vm((576, C), bf16),
        vm((4, WIN, C), bf16),
        vm((4, WIN, 3 * C), bf16),
        vm((4, WIN, 3 * C), bf16),
        vm((4, WIN, C), bf16),
        vm((C, 768), f32),
        vm((2, 2, 48, 768), bf16),
        vm((2, 48, 768), bf16),
        vm((2, 48, 768), bf16),
        vm((48, 768), bf16),
        vm((4, 16, 768), bf16),
        vm((3, 16, 768), bf16),
        vm((16, 768), bf16),
        vm((2, 2, 4, 16, 768), bf16),
        vm((4, 80, 384), bf16),
        vm((3, 80, 384), bf16),
        vm((80, 384), bf16),
        vm((4, 80, 384), bf16),
    ] + [sem] * 12 + [four] * 2
    whole = pl.BlockSpec(memory_space=pltpu.VMEM)
    stored = pl.BlockSpec(memory_space=pl.ANY)
    order_map, order_back, spread_map, spread_back = maps
    gathered = pl.pallas_call(
        kernel,
        out_shape=(
            jax.ShapeDtypeStruct((6, 2, PAD, C), bf16),
            jax.ShapeDtypeStruct((2, 2, 4, 16, 768), bf16),
            jax.ShapeDtypeStruct((4, 80, 384), bf16),
        ),
        in_specs=[stored] * 9 + [whole],
        out_specs=[whole] * 3,
        scratch_shapes=scratch,
        compiler_params=pltpu.CompilerParams(
            collective_id=0, has_side_effects=True, vmem_limit_bytes=VMEM_BYTES
        ),
    )(
        turned(attn_input), turned(out_grad), table, spread_map, order_map,
        w_qkv, w_proj, spread_back, order_back, codes,
    )
    grad_input, grad_qkv, grad_proj, folded = pl.pallas_call(
        functools.partial(finish, cells ** (-0.5)),
        out_shape=(
            jax.ShapeDtypeStruct((6, 2, PAD, C), bf16),
            jax.ShapeDtypeStruct((C, 3 * C), f32),
            jax.ShapeDtypeStruct((C, C), f32),
            jax.ShapeDtypeStruct((3456, 23), f32),
        ),
        in_specs=[stored] * 3,
        out_specs=[whole] * 4,
        scratch_shapes=[
            vm((2, 2, 4, 16, 768), bf16),
            vm((4, 80, 384), bf16),
            pltpu.SemaphoreType.DMA((3,)),
        ],
        compiler_params=pltpu.CompilerParams(vmem_limit_bytes=VMEM_BYTES),
    )(*gathered)
    grad_input = grad_input.reshape(6, 12, 8, C).transpose(2, 0, 1, 3)
    folded = folded.reshape(4, 1, 6, 2, 6, 6, 2, 23)
    return grad_input, grad_qkv, grad_proj, folded.transpose(0, 1, 2, 3, 6, 4, 5, 7)


def fitting_body(attn_input, *others):
    tuned = (
        lax.axis_size("lon") == 4
        and lax.axis_size("lat") == 4
        and attn_input.shape == (8, 6, 12, C)
    )
    return (fused_body if tuned else body)(attn_input, *others)


PAD = 48
VMEM_BYTES = 60 * 1024 * 1024


def solution(mesh):
    placed = (
        P("batch", "lat", "lon", None),
        P("batch", "lat", "lon", None),
        P(),
        P(),
        P(None, "lat", None, None, None, None, None, None),
        P("batch", "lat", "lon"),
        P("batch"),
    )
    return jax.shard_map(
        fitting_body,
        mesh=mesh,
        in_specs=placed,
        out_specs=(
            P("batch", "lat", "lon", None),
            P("batch", None),
            P("batch", None),
            P("batch", "lat", None, None, None, None, None, None),
        ),
        check_vma=False,
    )
```

```python
import functools

import jax
import jax.numpy as jnp
import numpy as np
from jax import lax
from jax.experimental import pallas as pl
from jax.experimental.pallas import tpu as pltpu
from jax.sharding import PartitionSpec as P

C = 192
HEADS = 6
HEAD_DIM = 32
WZ = 2
WLAT = 6
WLON = 12
WIN = 144


masked_score = -1000000000.0


def from_behind(shard, axis, by):
    devices = lax.axis_size(axis)
    return lax.ppermute(shard, axis, [(i, (i + by) % devices) for i in range(devices)])


def shifted_2(shard, axis, by):
    devices = lax.axis_size(axis)
    pairs = [(i, i + by) for i in range(devices) if 0 <= i + by < devices]
    return lax.ppermute(shard, axis, pairs)


def lon_table():
    column = jnp.arange(WLON, dtype=jnp.int32)
    offset = jnp.arange(2 * WLON - 1, dtype=jnp.int32)
    return (
        column[:, None, None] - column[None, :, None] + (WLON - 1) == offset[None, None, :]
    ).astype(jnp.float32)


def expand_bias(folded):
    expanded = jnp.einsum(
        "...hxyuvr,abr->...hxuayvb", folded, lon_table(), precision=lax.Precision.HIGHEST
    )
    return expanded.reshape(expanded.shape[:-7] + (HEADS, WIN, WIN))


def fold_bias(grads):
    divided = grads.reshape(grads.shape[:-3] + (HEADS, WZ, WLAT, WLON, WZ, WLAT, WLON))
    return jnp.einsum(
        "...hxuayvb,abr->...hxyuvr", divided, lon_table(), precision=lax.Precision.HIGHEST
    )


def to_windows(grid_field):
    levels, lat_rows, lon_cols = grid_field.shape[:3]
    trailing = grid_field.shape[3:]
    divided = grid_field.reshape(
        (levels // WZ, WZ, lat_rows // WLAT, WLAT, lon_cols // WLON, WLON) + trailing
    )
    arrangement = (0, 2, 4, 1, 3, 5) + tuple(range(6, 6 + len(trailing)))
    return divided.transpose(arrangement).reshape(
        (levels // WZ, lat_rows // WLAT, lon_cols // WLON, WIN) + trailing
    )


def from_windows(windows, levels, lat_rows, lon_cols):
    trailing = windows.shape[4:]
    divided = windows.reshape(
        (levels // WZ, lat_rows // WLAT, lon_cols // WLON, WZ, WLAT, WLON) + trailing
    )
    arrangement = (0, 3, 1, 4, 2, 5) + tuple(range(6, 6 + len(trailing)))
    return divided.transpose(arrangement).reshape((levels, lat_rows, lon_cols) + trailing)


def outer_part(grid_field, cut_width, axis, leading):
    length = grid_field.shape[axis]
    if leading:
        return lax.slice_in_dim(grid_field, 0, cut_width, axis=axis)
    return lax.slice_in_dim(grid_field, length - cut_width, length, axis=axis)


def inner_part(grid_field, cut_width, axis, leading):
    length = grid_field.shape[axis]
    if leading:
        return lax.slice_in_dim(grid_field, cut_width, length, axis=axis)
    return lax.slice_in_dim(grid_field, 0, length - cut_width, axis=axis)


def attach(kept, arrived, axis, leading):
    if leading:
        return jnp.concatenate([kept, arrived], axis=axis)
    return jnp.concatenate([arrived, kept], axis=axis)


def displace(fields, heading):
    leading = heading < 0
    fields = [jnp.roll(grid_field, heading * (WZ // 2), axis=0) for grid_field in fields]
    border = jnp.stack([outer_part(grid_field, WLON // 2, 2, leading) for grid_field in fields])
    arrived = from_behind(border, "lon", heading)
    fields = [
        attach(inner_part(grid_field, WLON // 2, 2, leading), arrived[number], 2, leading)
        for number, grid_field in enumerate(fields)
    ]
    border = jnp.stack([outer_part(grid_field, WLAT // 2, 1, leading) for grid_field in fields])
    arrived = shifted_2(border, "lat", heading)
    return [
        attach(inner_part(grid_field, WLAT // 2, 1, leading), arrived[number], 1, leading)
        for number, grid_field in enumerate(fields)
    ]


def window_backward(shifted, grads_y, allowed, bias, w_qkv, w_proj):
    groups = shifted.shape[0]
    flattened = shifted.reshape(groups * WIN, C)
    projected = jnp.dot(flattened, w_qkv, preferred_element_type=jnp.float32).astype(jnp.bfloat16)
    projected = projected.reshape(groups, WIN, 3, HEADS, HEAD_DIM)
    query_rows = projected[:, :, 0]
    key_rows = projected[:, :, 1]
    value_rows = projected[:, :, 2]
    temper = HEAD_DIM ** (-0.5)
    scores = (
        jnp.einsum("gnhd,gmhd->ghnm", query_rows, key_rows, preferred_element_type=jnp.float32)
        * temper
        + bias
    )
    scores = jnp.where(allowed[:, None], scores, masked_score)
    exponent = jnp.exp(scores - jnp.max(scores, axis=-1, keepdims=True))
    attn_probs = exponent / jnp.sum(exponent, axis=-1, keepdims=True)
    probs_low = attn_probs.astype(jnp.bfloat16)
    attended = jnp.einsum(
        "ghnm,gmhd->gnhd", probs_low, value_rows, preferred_element_type=jnp.float32
    )
    attended = attended.astype(jnp.bfloat16).reshape(groups * WIN, C)
    upstream = grads_y.reshape(groups * WIN, C)
    grad_proj = jnp.einsum("tc,te->ce", attended, upstream, preferred_element_type=jnp.float32)
    grad_att = jnp.einsum("te,ce->tc", upstream, w_proj, preferred_element_type=jnp.float32)
    grad_att = grad_att.astype(jnp.bfloat16).reshape(groups, WIN, HEADS, HEAD_DIM)
    grad_prob = jnp.einsum(
        "gnhd,gmhd->ghnm", grad_att, value_rows, preferred_element_type=jnp.float32
    )
    grad_score = attn_probs * (grad_prob - jnp.sum(attn_probs * grad_prob, axis=-1, keepdims=True))
    scaled = (grad_score * temper).astype(jnp.bfloat16)
    grad_query = jnp.einsum("ghnm,gmhd->gnhd", scaled, key_rows, preferred_element_type=jnp.float32)
    grad_key = jnp.einsum("ghnm,gnhd->gmhd", scaled, query_rows, preferred_element_type=jnp.float32)
    grad_value = jnp.einsum(
        "ghnm,gnhd->gmhd", probs_low, grad_att, preferred_element_type=jnp.float32
    )
    grad_rows = (
        jnp.stack([grad_query, grad_key, grad_value], axis=2)
        .astype(jnp.bfloat16)
        .reshape(groups * WIN, 3 * C)
    )
    weight_qkv = jnp.einsum("tc,te->ce", flattened, grad_rows, preferred_element_type=jnp.float32)
    grad_shifted = jnp.einsum(
        "te,ce->tc", grad_rows, w_qkv, preferred_element_type=jnp.float32
    ).astype(jnp.bfloat16)
    return (grad_shifted.reshape(groups, WIN, C), weight_qkv, grad_proj, grad_score)


def body(attn_input, out_grad, w_qkv, w_proj, bias_table, mask_ids, valid_rows):
    levels, lat_rows, lon_cols, channels = attn_input.shape
    moved_input, moved_grad = displace([attn_input, out_grad], -1)
    shifted = to_windows(moved_input)
    grads_y = to_windows(moved_grad)
    anchor = jnp.arange(lat_rows, dtype=jnp.int32) + lax.axis_index("lat") * lat_rows + WLAT // 2
    usable = jnp.broadcast_to((anchor < valid_rows[0])[None, :, None], (levels, lat_rows, lon_cols))
    regions = to_windows(mask_ids)
    usable_win = to_windows(usable)
    allowed = (regions[..., :, None] == regions[..., None, :]) & usable_win[..., None, :]
    allowed = allowed | jnp.eye(WIN, dtype=bool)
    bias_full = expand_bias(bias_table)
    level_wins, lat_wins, lon_wins = shifted.shape[:3]

    def regroup(windows):
        rotated = jnp.moveaxis(windows, 1, 0)
        return rotated.reshape((lat_wins, level_wins * lon_wins) + windows.shape[3:])

    def one_band(pieces):
        band_input, band_grads, band_mask, band_bias = pieces
        expanded = band_bias[:, None]
        expanded = expanded.reshape(level_wins * lon_wins, HEADS, WIN, WIN)
        grad_in, weight_qkv, weight_proj, grad_score = window_backward(
            band_input, band_grads, band_mask, expanded, w_qkv, w_proj
        )
        folded = fold_bias(
            jnp.sum(grad_score.reshape(level_wins, lon_wins, HEADS, WIN, WIN), axis=1)
        )
        return (grad_in, weight_qkv, weight_proj, folded)

    grad_in, weight_qkv, weight_proj, folded = lax.map(
        one_band,
        (regroup(shifted), regroup(grads_y), regroup(allowed), jnp.moveaxis(bias_full, 1, 0)),
    )
    grad_in = jnp.moveaxis(grad_in.reshape((lat_wins, level_wins, lon_wins, WIN, channels)), 0, 1)
    grad_input = displace([from_windows(grad_in, levels, lat_rows, lon_cols)], 1)[0]
    local_qkv = jnp.sum(weight_qkv, axis=0)
    local_proj = jnp.sum(weight_proj, axis=0)
    local_table = jnp.moveaxis(folded, 0, 1)
    total_qkv, total_proj = lax.psum((local_qkv, local_proj), ("lon", "lat"))
    grad_bias = lax.psum(local_table, "lon")
    cells = levels * lat_rows * lax.axis_size("lat") * lon_cols * lax.axis_size("lon")
    factor = cells ** (-0.5)
    return (grad_input, total_qkv * factor, total_proj * factor, grad_bias)

def place_map():
    order = np.zeros((576, 576), np.float32)
    for i in range(4):
        for c in range(12):
            for a in range(2):
                for b in range(6):
                    order[i * WIN + c * 12 + a * 6 + b, b * 96 + c * 8 + (2 * i + a + 1) % 8] = 1.0
    return order


def bias_map():
    spread = np.zeros((384, 384), np.float32)
    for a in range(2):
        for b in range(6):
            for d in range(23):
                spread[(2 * b + a) * 32 + d, (22 - d) * 12 + a * 6 + b] = 1.0
    return spread


def dot_nn(a, b):
    return lax.dot_general(a, b, (((1,), (0,)), ((), ())), preferred_element_type=jnp.float32)


def dot_nt(a, b):
    return lax.dot_general(a, b, (((1,), (1,)), ((), ())), preferred_element_type=jnp.float32)


def dot_tn(a, b):
    return lax.dot_general(a, b, (((0,), (0,)), ((), ())), preferred_element_type=jnp.float32)


def kernel(
    x_hbm, g_hbm, tab_hbm, gm_hbm, pm_hbm, wq_hbm, wp_hbm, gmt_hbm, pt_hbm, ids_ref,
    out_x, out_w, out_b,
    x_ref, g_ref, tab_ref, gm_ref, pm_ref, wq_ref, wp_ref, gmt_ref, pt_ref, fetch_sem,
    pk, sg, hs, og, bias, tabx, tp, fold, dsr, xa, ga, aa, gr, qa, ca, dw,
    ws, wr1, w2, wr2, wl, wm, wf, wo, bs, br, bg, bo,
    halo_send, halo_recv, back_send, back_recv, bsum_send, bsum_recv, ball_send, ball_recv,
    wb_send, wb_recv, wc_send, wc_recv, pair_send, pair_recv,
):
    f32, bf16 = jnp.float32, jnp.bfloat16
    lon, lat = lax.axis_index("lon"), lax.axis_index("lat")
    nl, nt = 4, 4
    core, far_y = lax.rem(lat, 2), lat // 2

    def at(dlon, dlat):
        return {"lon": lax.rem(lon + dlon + nl, nl), "lat": lax.rem(lat + dlat + nt, nt)}

    def remote(src, dst, send, recv, where):
        return pltpu.make_async_remote_copy(
            src_ref=src, dst_ref=dst, send_sem=send, recv_sem=recv,
            device_id=where, device_id_type=pl.DeviceIdType.MESH,
        )

    fetches = [
        pltpu.make_async_copy(src, dst, fetch_sem.at[n])
        for n, (src, dst) in enumerate(
            (
                (x_hbm, x_ref), (g_hbm, g_ref), (tab_hbm, tab_ref), (gm_hbm, gm_ref),
                (pm_hbm, pm_ref), (wq_hbm, wq_ref), (wp_hbm, wp_ref), (gmt_hbm, gmt_ref),
                (pt_hbm, pt_ref),
            )
        )
    ]
    for fetch in fetches:
        fetch.start()
    barrier = pltpu.get_barrier_semaphore()
    friends = [(1, 0), (2, 0), (3, 0), (0, 1), (0, 2), (0, 3), (1, 1), (-1, -1)]
    for dlon, dlat in friends:
        pl.semaphore_signal(
            barrier, inc=1, device_id=at(dlon, dlat), device_id_type=pl.DeviceIdType.MESH
        )

    fetches[0].wait()
    fetches[1].wait()
    pk[:, :, :, 0:C] = x_ref[...]
    pk[:, :, :, C : 2 * C] = g_ref[...]
    sg[0:3, 0] = pk[3:6, 1]
    pl.semaphore_wait(barrier, len(friends))
    halo = [
        remote(pk.at[pl.ds(3, 3), 0], sg.at[pl.ds(0, 3), 1], halo_send.at[0], halo_recv.at[0], at(-1, 0)),
        remote(pk.at[pl.ds(0, 3), 0], sg.at[pl.ds(3, 3), 1], halo_send.at[2], halo_recv.at[2], at(-1, -1)),
        remote(pk.at[pl.ds(0, 3), 1], sg.at[pl.ds(3, 3), 0], halo_send.at[1], halo_recv.at[1], at(0, -1)),
    ]
    for copy in halo:
        copy.start()

    tabx[...] = jnp.zeros_like(tabx)
    for fetch in fetches[2:]:
        fetch.wait()
    for p in range(12):
        tabx[:, 32 * p : 32 * p + 23] = tab_ref[pl.ds(p, 288, stride=12), :]
    table = tabx[...]
    top = table.astype(bf16)
    rest = table - top.astype(f32)
    mid = rest.astype(bf16)
    low_part = (rest - mid.astype(f32)).astype(bf16)
    spread = gm_ref[...]
    spreaded = dot_nn(top, spread) + dot_nn(mid, spread) + dot_nn(low_part, spread)
    for i in range(4):
        tp[i] = spreaded[72 * i : 72 * i + 72]

    def expand(i, carry):
        for h in range(HEADS):
            for c in range(12):
                bias[i, h, 12 * c : 12 * c + 12, :] = tp[
                    i, 12 * h : 12 * h + 12, 12 * (11 - c) : 12 * (11 - c) + WIN
                ]
        return carry

    lax.fori_loop(0, 4, expand, 0)
    for n in range(4):
        wl[n] = jnp.zeros((16, 768), bf16)
    spot = lax.broadcasted_iota(jnp.int32, (1, 576), 1)
    keep = jnp.where((spot >= 288) & (lat == nt - 1), 0.0, 1.0).astype(bf16)
    pm = pm_ref[...] * keep
    rows = lax.broadcasted_iota(jnp.int32, (WIN, WIN), 0)
    cols = lax.broadcasted_iota(jnp.int32, (WIN, WIN), 1)
    same = rows == cols
    for copy in halo:
        copy.wait()

    both = dot_nn(pm, sg[...].reshape(576, 2 * C)).astype(bf16)
    xs = both[:, :C]
    gs_all = both[:, C:]
    xa[...] = xs
    ga[...] = gs_all
    qkv_all = dot_nn(xs, wq_ref[...]).astype(bf16)
    gatt_all = dot_nt(gs_all, wp_ref[...]).astype(bf16)
    for i in range(4):
        qa[i] = qkv_all[WIN * i : WIN * i + WIN]
        ca[i] = gatt_all[WIN * i : WIN * i + WIN]
    temper = HEAD_DIM ** (-0.5)
    lane = lax.broadcasted_iota(jnp.int32, (WIN, 8), 1)

    def bias_copy(s):
        w = lax.rem(lon + 1 + s, nl)
        return remote(bs.at[w], br.at[s], bsum_send.at[s], bsum_recv.at[s], at(1 + s, 0))

    def window(s, carry):
        w = lax.rem(lon + 1 + s, nl)
        code = ids_ref[w]
        usable = code >= 4
        region = jnp.where(usable, code - 4, code)
        hot = jnp.where(region == lane, 1.0, 0.0).astype(bf16)
        keyed = jnp.where(usable & (region == lane), 1.0, 0.0).astype(bf16)
        allowed = (dot_nt(hot, keyed) > 0.5) | same
        fold[...] = jnp.zeros_like(fold)
        held = []
        for h in range(HEADS):
            lo = HEAD_DIM * h
            q = qa[w, :, lo : lo + 32]
            k = qa[w, :, C + lo : C + lo + 32]
            v = qa[w, :, 2 * C + lo : 2 * C + lo + 32]
            go = ca[w, :, lo : lo + 32]
            held.append((q, k, v, go, dot_nt(q, k), dot_nt(go, v)))
        ready = []
        for h, (q, k, v, go, raw, gp) in enumerate(held):
            scores = jnp.where(allowed, raw * temper + bias[w, h], masked_score)
            power = jnp.exp(scores - jnp.max(scores, axis=-1, keepdims=True))
            probs = power * (1.0 / jnp.sum(power, axis=-1, keepdims=True))
            gs = probs * (gp - jnp.sum(probs * gp, axis=-1, keepdims=True))
            dsr[h] = gs
            ready.append((probs.astype(bf16), (gs * temper).astype(bf16)))
        for h, (low, scaled) in enumerate(ready):
            q, k, v, go = held[h][:4]
            lo = HEAD_DIM * h
            aa[w, :, lo : lo + 32] = dot_nn(low, v).astype(bf16)
            gr[w, :, lo : lo + 32] = dot_nn(scaled, k).astype(bf16)
            gr[w, :, C + lo : C + lo + 32] = dot_tn(scaled, q).astype(bf16)
            gr[w, :, 2 * C + lo : 2 * C + lo + 32] = dot_tn(low, go).astype(bf16)
            for c in range(12):
                off = 12 * (11 - c)
                fold[12 * h : 12 * h + 12, off : off + WIN] += dsr[h, 12 * c : 12 * c + 12, :]
        bs[w] = dot_nn(fold[...].astype(bf16), gmt_ref[...]).astype(bf16)

        @pl.when(s < 3)
        def _():
            bias_copy(s).start()

        return carry

    lax.fori_loop(0, 4, window, 0, unroll=True)

    grads = gr[...].reshape(576, 576)
    dw[:, :576] = dot_tn(xa[...], grads)
    dw[:, 576:] = dot_tn(aa[...].reshape(576, C), ga[...])
    for n in range(4):
        ws[n % 2, n // 2] = dw[48 * n : 48 * n + 48, :].astype(bf16)
    mate = {"lat": lat + 1 - 2 * core}
    first = remote(ws.at[1 - core], wr1, pair_send.at[0], pair_recv.at[0], mate)
    first.start()

    back = dot_nt(grads, wq_ref[...]).astype(bf16)
    hs[...] = dot_nn(pt_ref[...], back).astype(bf16).reshape(6, 2, PAD, C)

    first.wait()
    w2[...] = (ws[core].astype(f32) + wr1[...].astype(f32)).astype(bf16)
    across = {"lat": lax.rem(lat + 2, nt)}
    second = remote(w2.at[1 - far_y], wr2, pair_send.at[1], pair_recv.at[1], across)
    second.start()
    home = [
        remote(hs.at[pl.ds(0, 3), 1], og.at[pl.ds(3, 3), 0], back_send.at[0], back_recv.at[0], at(1, 0)),
        remote(hs.at[pl.ds(3, 3), 1], og.at[pl.ds(0, 3), 0], back_send.at[2], back_recv.at[2], at(1, 1)),
        remote(hs.at[pl.ds(3, 3), 0], og.at[pl.ds(0, 3), 1], back_send.at[1], back_recv.at[1], at(0, 1)),
    ]

    for copy in home:
        copy.start()
    for s in range(3):
        bias_copy(s).wait()
    total = bs[lon].astype(f32)
    for s in range(3):
        total = total + br[s].astype(f32)
    bg[...] = total.astype(bf16)

    second.wait()
    part_sum = w2[far_y].astype(f32) + wr2[...].astype(f32)
    dw[0:48, :] = part_sum
    for n in range(4):
        wl[n, 0:12, :] = dw[12 * n : 12 * n + 12, :].astype(bf16)
    wb = []
    for d in range(1, 4):
        to = lax.rem(lon + d, nl)
        wb.append(
            remote(wl.at[to], wm.at[d - 1], wb_send.at[d - 1], wb_recv.at[d - 1], at(d, 0))
        )
    for copy in wb:
        copy.start()
    ball = [
        remote(bg, bo.at[lon], ball_send.at[d - 1], ball_recv.at[d - 1], at(d, 0))
        for d in range(1, 4)
    ]

    og[3:6, 1] = hs[0:3, 0]
    bo[lon] = bg[...]
    for copy in wb:
        copy.wait()
    mine = wl[lon].astype(f32)
    for d in range(3):
        mine = mine + wm[d].astype(f32)
    wf[...] = mine.astype(bf16)
    wo[core, far_y, lon] = wf[...]
    wc = [
        remote(wf, wo.at[core, far_y, lon], wc_send.at[d - 1], wc_recv.at[d - 1], at(d, 0))
        for d in range(1, 4)
    ]
    for copy in wc:
        copy.start()
    for copy in ball:
        copy.start()
    for copy in wc:
        copy.wait()
    own = wo.at[core, far_y]
    third = remote(own, own, pair_send.at[2], pair_recv.at[2], across)
    third.start()

    for copy in home:
        copy.wait()
    fill = jnp.where(lat == 0, 0.0, 1.0).astype(bf16)
    out_x[0:3] = og[0:3] * fill
    out_x[3:6] = og[3:6]

    third.wait()
    half = wo.at[core]
    fourth = remote(half, half, pair_send.at[3], pair_recv.at[3], mate)
    fourth.start()

    for copy in ball:
        copy.wait()
    out_b[...] = bo[...]
    fourth.wait()
    out_w[...] = wo[...]


def finish(factor, og_hbm, wo_hbm, bo_hbm, out_x, out_w, out_p, out_b, wo, bo, sems):
    f32 = jnp.float32
    fetches = [
        pltpu.make_async_copy(src, dst, sems.at[n])
        for n, (src, dst) in enumerate(((bo_hbm, bo), (wo_hbm, wo), (og_hbm, out_x)))
    ]
    for fetch in fetches:
        fetch.start()
    fetches[0].wait()
    for i in range(4):
        piece = bo[i].astype(f32)
        for p in range(12):
            out_b[pl.ds(864 * i + p, 72, stride=12), :] = piece[0:72, 32 * p : 32 * p + 23]
    fetches[1].wait()
    for n in range(16):
        piece = wo[(n // 4) % 2, n // 8, n % 4].astype(f32) * factor
        out_w[12 * n : 12 * n + 12, :] = piece[0:12, :576]
        out_p[12 * n : 12 * n + 12, :] = piece[0:12, 576:]
    fetches[2].wait()


def fused_body(attn_input, out_grad, w_qkv, w_proj, bias_table, mask_ids, valid_rows):
    f32, bf16 = jnp.float32, jnp.bfloat16
    levels, lat_rows, lon_cols, _ = attn_input.shape
    anchor = jnp.arange(lat_rows, dtype=jnp.int32) + lax.axis_index("lat") * lat_rows + WLAT // 2
    usable = (anchor < valid_rows[0])[None, :, None]
    codes = jnp.where(usable, mask_ids + 4, mask_ids)
    codes = codes.reshape(4, 2, 6, 12).transpose(0, 3, 1, 2).reshape(4, WIN, 1)
    table = bias_table.transpose(0, 1, 2, 3, 5, 6, 4, 7).reshape(3456, 23)

    def turned(field):
        return field.transpose(1, 2, 0, 3).reshape(6, 2, PAD, C)

    order = place_map()
    spread = bias_map()
    maps = [jnp.asarray(m, bf16) for m in (order, order.T, spread, spread.T)]
    cells = levels * lat_rows * lax.axis_size("lat") * lon_cols * lax.axis_size("lon")
    vm = pltpu.VMEM
    sem = pltpu.SemaphoreType.DMA((3,))
    four = pltpu.SemaphoreType.DMA((4,))
    scratch = [
        vm((6, 2, PAD, C), bf16),
        vm((6, 2, PAD, C), bf16),
        vm((3456, 23), f32),
        vm((384, 384), bf16),
        vm((576, 576), bf16),
        vm((C, 3 * C), bf16),
        vm((C, C), bf16),
        vm((384, 384), bf16),
        vm((576, 576), bf16),
        pltpu.SemaphoreType.DMA((9,)),
        vm((6, 2, PAD, 2 * C), bf16),
        vm((6, 2, PAD, 2 * C), bf16),
        vm((6, 2, PAD, C), bf16),
        vm((6, 2, PAD, C), bf16),
        vm((4, HEADS, WIN, WIN), f32),
        vm((288, 384), f32),
        vm((4, 72, 384), f32),
        vm((80, 384), f32),
        vm((HEADS, WIN, WIN), f32),
        vm((576, C), bf16),
        vm((576, C), bf16),
        vm((4, WIN, C), bf16),
        vm((4, WIN, 3 * C), bf16),
        vm((4, WIN, 3 * C), bf16),
        vm((4, WIN, C), bf16),
        vm((C, 768), f32),
        vm((2, 2, 48, 768), bf16),
        vm((2, 48, 768), bf16),
        vm((2, 48, 768), bf16),
        vm((48, 768), bf16),
        vm((4, 16, 768), bf16),
        vm((3, 16, 768), bf16),
        vm((16, 768), bf16),
        vm((2, 2, 4, 16, 768), bf16),
        vm((4, 80, 384), bf16),
        vm((3, 80, 384), bf16),
        vm((80, 384), bf16),
        vm((4, 80, 384), bf16),
    ] + [sem] * 12 + [four] * 2
    whole = pl.BlockSpec(memory_space=pltpu.VMEM)
    stored = pl.BlockSpec(memory_space=pl.ANY)
    order_map, order_back, spread_map, spread_back = maps
    gathered = pl.pallas_call(
        kernel,
        out_shape=(
            jax.ShapeDtypeStruct((6, 2, PAD, C), bf16),
            jax.ShapeDtypeStruct((2, 2, 4, 16, 768), bf16),
            jax.ShapeDtypeStruct((4, 80, 384), bf16),
        ),
        in_specs=[stored] * 9 + [whole],
        out_specs=[whole] * 3,
        scratch_shapes=scratch,
        compiler_params=pltpu.CompilerParams(
            collective_id=0, has_side_effects=True, vmem_limit_bytes=VMEM_BYTES
        ),
    )(
        turned(attn_input), turned(out_grad), table, spread_map, order_map,
        w_qkv, w_proj, spread_back, order_back, codes,
    )
    grad_input, grad_qkv, grad_proj, folded = pl.pallas_call(
        functools.partial(finish, cells ** (-0.5)),
        out_shape=(
            jax.ShapeDtypeStruct((6, 2, PAD, C), bf16),
            jax.ShapeDtypeStruct((C, 3 * C), f32),
            jax.ShapeDtypeStruct((C, C), f32),
            jax.ShapeDtypeStruct((3456, 23), f32),
        ),
        in_specs=[stored] * 3,
        out_specs=[whole] * 4,
        scratch_shapes=[
            vm((2, 2, 4, 16, 768), bf16),
            vm((4, 80, 384), bf16),
            pltpu.SemaphoreType.DMA((3,)),
        ],
        compiler_params=pltpu.CompilerParams(vmem_limit_bytes=VMEM_BYTES),
    )(*gathered)
    grad_input = grad_input.reshape(6, 12, 8, C).transpose(2, 0, 1, 3)
    folded = folded.reshape(4, 1, 6, 2, 6, 6, 2, 23)
    return grad_input, grad_qkv, grad_proj, folded.transpose(0, 1, 2, 3, 6, 4, 5, 7)


def fitting_body(attn_input, *others):
    tuned = (
        lax.axis_size("lon") == 4
        and lax.axis_size("lat") == 4
        and attn_input.shape == (8, 6, 12, C)
    )
    return (fused_body if tuned else body)(attn_input, *others)


PAD = 48
VMEM_BYTES = 60 * 1024 * 1024


def solution(mesh):
    placed = (
        P("batch", "lat", "lon", None),
        P("batch", "lat", "lon", None),
        P(),
        P(),
        P(None, "lat", None, None, None, None, None, None),
        P("batch", "lat", "lon"),
        P("batch"),
    )
    return jax.shard_map(
        fitting_body,
        mesh=mesh,
        in_specs=placed,
        out_specs=(
            P("batch", "lat", "lon", None),
            P("batch", None),
            P("batch", None),
            P("batch", "lat", None, None, None, None, None, None),
        ),
        check_vma=False,
    )
```
